512 devices in a mesh: docs: 64 (over y, z), dim: 8 (over x, core).
Axes of the slice: x: 4, y: 4, z: 16, core: 2. Of those that a mesh axis runs over, the one named last changes fastest.
Arguments:
- sketches: bfloat16 [32768, 8192], P('docs', 'dim'), may hold values from -1.5 to 1.5
- clusters: int32 [32768], P('docs'), may hold values from 0 to 4095, as said below
- queries: bfloat16 [1024, 8192], P(None, 'dim'), may hold values from -6 to 6
Outputs:
- gram: float32 [4096, 4096], P(('docs', 'dim'))
- scores: float32 [4096, 1024], P(('docs', 'dim'))
The draws below stay inside these ranges and needn't reach their ends.
Inputs may be any that keep to these rules, and one draw needn't show every extreme that they name: Cluster c is owned by docs index c // 64. Among the documents of one index of docs (aligned blocks of 512), at most 32 belong to clusters of one owner, and in every block some owner gets exactly 32.
All inputs are finite; a program needn't handle non-finite values.
Results may differ from the reference program's by a relative error of at most 0.0029.
Values may be sent and summed in bfloat16 or wider, within the bound.
A program may use at most 64 MiB of HBM per device.

```python
import jax
import jax.numpy as jnp
from jax import lax

K = 8192
CL_DEV = 64
NQ = 1024
DOC_DEV = 512
CAP = 32
CLUSTERS = 4096
DOCS = 32768
N_DOCS = 64


def draw_clusters(key, part):
    key = jax.random.fold_in(key, 5)
    keys = jax.random.split(key, 6)
    position_count = N_DOCS * CAP
    position_holder = jnp.arange(position_count, dtype=jnp.int32) // CAP
    base = jax.random.randint(keys[0], (N_DOCS,), 0, 1 << 7)
    holder_bias = (base * base).astype(jnp.int32)
    dominant_weight = jax.random.randint(keys[1], (N_DOCS,), 0, N_DOCS)
    random_jitter = jax.random.randint(keys[2], (N_DOCS, position_count), 0, 1 << 14)
    extra_reward = jnp.where(position_holder[None, :] == dominant_weight[:, None], 1 << 15, 0).astype(jnp.int32)
    match_score = (random_jitter + holder_bias[position_holder][None, :] + extra_reward) * 16384 + jnp.arange(position_count, dtype=jnp.int32)[None, :]
    chosen = lax.top_k(match_score, DOC_DEV)[1].astype(jnp.int32)
    owners = chosen // CAP
    perms = jax.vmap(lambda k: jax.random.permutation(k, DOC_DEV))(jax.random.split(keys[3], N_DOCS))
    owners = jnp.take_along_axis(owners, perms.astype(jnp.int32), axis=1)
    raw = jax.random.randint(keys[4], (N_DOCS, DOC_DEV), 0, CL_DEV * 64)
    local_index = raw * raw // (CL_DEV * 4096)
    rotation = jax.random.randint(keys[5], (N_DOCS,), 0, CL_DEV)
    local_index = (local_index + rotation[owners]) % CL_DEV
    return (owners * CL_DEV + local_index).reshape(-1).astype(jnp.int32)


def level_of(own_key, dims, cuts, least, largest):
    level = 1.0
    for axis_at, blocks in cuts:
        heights = jax.random.uniform(jax.random.fold_in(jax.random.fold_in(own_key, 6), axis_at), (blocks,), jnp.float32, least / len(cuts), largest / len(cuts))
        level = level * jnp.repeat(jnp.exp(heights), dims[axis_at] // blocks).reshape((-1,) + (1,) * (len(dims) - 1 - axis_at))
    return level


def gaussian(key, shape, width, reach, pieces=(), held_as=jnp.bfloat16):
    loudness = level_of(key, shape, pieces, -0.22, 0.18) if pieces else 1.0
    result = jax.random.normal(key, shape, jnp.float32) * width * loudness
    return jnp.minimum(jnp.maximum(result, -reach), reach).astype(held_as)


def setup_inputs(seed: int = 0) -> dict:
    arg_keys = jax.random.split(jax.random.key(seed), 4)
    sketches = gaussian(arg_keys[0], (DOCS, K), 0.25, 1.5, ((0, 64), (1, 8)))
    clusters = draw_clusters(jax.random.fold_in(arg_keys[3], 71), 0)
    queries = gaussian(arg_keys[2], (NQ, K), 1.0, 6.0, ((1, 8),))
    return {"sketches": sketches, "clusters": clusters, "queries": queries}


def reference(sketches, clusters, queries):
    summed = jax.ops.segment_sum(sketches.astype(jnp.float32), clusters, num_segments=CLUSTERS).astype(jnp.bfloat16)
    gram = jnp.dot(summed, summed.T, preferred_element_type=jnp.float32) * (1.0 / K)
    scores = jnp.dot(summed, queries.T, preferred_element_type=jnp.float32) * (K ** -0.5)
    return gram, scores
```

```python
import functools
import math

import jax
import jax.numpy as jnp
from jax import lax
from jax.experimental import pallas as pl
from jax.experimental.pallas import tpu as pltpu
from jax.sharding import PartitionSpec as P

MESH = pl.DeviceIdType.MESH
CL = 64
NY = 4
LN2 = math.log(2.0)
BITS = 15


def power(level):
    return jnp.exp(level * LN2).astype(jnp.bfloat16).astype(jnp.float32)


def quantise(part):
    peak = jnp.maximum(jnp.max(jnp.abs(part), axis=0, keepdims=True), 1e-30)
    level = jnp.floor(jnp.log(peak) * (1.0 / LN2) + 0.001) + 1.0
    values = jnp.round(part * power(BITS - level)).astype(jnp.int32).astype(jnp.int16)
    levels = jnp.broadcast_to(level, (16, part.shape[1])).astype(jnp.int32).astype(jnp.int16)
    return values, levels


def restore(values, levels):
    level = levels.astype(jnp.int32).astype(jnp.float32)[0:1]
    return values.astype(jnp.int32).astype(jnp.float32) * power(level - BITS)


def kernel(
    sizes, sk_ref, ids_ref, qu_ref, gram_ref, scores_ref,
    docs_in, ids_in, quer, zpos, row, acc, rs_out, rs_in, own_cols, cols, rows,
    part, pair_in, half, x_in, done, y_in, s_part, s_pair_in, s_half, s_x_in,
    local_sem, a_ss, a_rs, i_ss, i_rs, rs_ss, rs_rs, c_ss, c_rs, r_ss, r_rs, g_ss, g_rs,
    p_ss, p_rs, x_ss, x_rs, f_ss, f_rs, sp_ss, sp_rs, sx_ss, sx_rs,
):
    ny, nz, nx, cl = sizes
    n_docs, kd = sk_ref.shape
    kq = kd // ny
    sub = kq // 2
    n_rows = ny * cl
    hops = nz // 2
    groups = nz // 2
    dims = 2 * nx

    docs_at = lax.axis_index("docs")
    dim_at = lax.axis_index("dim")
    y, z = docs_at // nz, docs_at % nz
    x, core = dim_at // 2, dim_at % 2

    def dev(yy, zz, xx, cc):
        return (yy * nz + zz, xx * 2 + cc)

    def y_peer(o):
        return dev((y + o) % ny, z, x, core)

    def x_peer(o):
        return dev(y, z, (x + o) % nx, core)

    z_next = (dev(y, (z + 1) % nz, x, core), dev(y, (z + nz - 1) % nz, x, core))
    mate = dev(y, z, x, 1 - core)

    def remote(src, dst, ssem, rsem, to):
        return pltpu.make_async_remote_copy(
            src_ref=src, dst_ref=dst, send_sem=ssem, recv_sem=rsem, device_id=to, device_id_type=MESH
        )

    own_docs = pltpu.make_async_copy(
        sk_ref.at[:, pl.ds(pl.multiple_of(y * kq, kq), kq)], docs_in.at[0], local_sem.at[0]
    )
    own_docs.start()
    own_quer = pltpu.make_async_copy(qu_ref, quer, local_sem.at[1])
    own_quer.start()

    barrier = pltpu.get_barrier_semaphore()
    partners = [y_peer(o) for o in range(1, ny)] + [x_peer(o) for o in range(1, nx)] + list(z_next) + [mate]
    for to in partners:
        pl.semaphore_signal(barrier, inc=1, device_id=to, device_id_type=MESH)
    pl.semaphore_wait(barrier, len(partners))

    def ids_copy(o):
        return remote(ids_ref, ids_in.at[o], i_ss.at[o], i_rs.at[o], y_peer(o))

    def docs_copy(o, h):
        at = pl.multiple_of(((y + o) % ny) * kq + h * sub, sub)
        return remote(
            sk_ref.at[:, pl.ds(at, sub)], docs_in.at[o, :, pl.ds(h * sub, sub)], a_ss.at[o, h], a_rs.at[o, h], y_peer(o)
        )

    for o in range(1, ny):
        ids_copy(o).start()
    for h in range(2):
        for o in range(1, ny):
            docs_copy(o, h).start()
    ids_in[0] = ids_ref[...]
    for o in range(1, ny):
        ids_copy(o).wait_recv()
    ids = ids_in[...]
    owner = lax.shift_right_logical(ids, int(math.log2(cl)))
    zpos[...] = lax.bitwise_and(owner, nz - 1)
    row[...] = lax.shift_right_logical(owner, int(math.log2(nz))) * cl + lax.bitwise_and(ids, cl - 1)
    own_docs.wait()
    for h in range(2):
        for o in range(1, ny):
            docs_copy(o, h).wait_recv()

    def onehot(target):
        places = lax.broadcasted_iota(jnp.int32, (n_rows, n_docs), 0)
        pieces = []
        for o in range(ny):
            here = jnp.where(zpos[o, 0:1, :] == target, row[o, 0:1, :], -1)
            pieces.append((here == places).astype(jnp.float32).astype(jnp.bfloat16))
        return jnp.concatenate(pieces, axis=1)

    def sums(targets):
        hot = [onehot(t) for t in targets]
        hot = jnp.concatenate(hot, axis=0) if len(hot) > 1 else hot[0]
        return jnp.dot(hot, docs_in[...].reshape(ny * n_docs, kq), preferred_element_type=jnp.float32)

    def rs_copy(way, h, s):
        return remote(
            rs_out.at[way, h, s], rs_in.at[way, h, s], rs_ss.at[way, h, s], rs_rs.at[way, h, s], z_next[way]
        )

    def rs_send(way, h, s, value):
        values, levels = quantise(value)
        rs_out[way, h, s, 0:n_rows] = values
        rs_out[way, h, s, n_rows : n_rows + 16] = levels
        rs_copy(way, h, s).start()

    def rs_got(way, h, s):
        rs_copy(way, h, s).wait_recv()
        return restore(rs_in[way, h, s, 0:n_rows], rs_in[way, h, s, n_rows : n_rows + 16])

    def fill(s):
        both = sums([(z + hops - s) % nz, (z + nz - hops + s) % nz])
        acc[0] = both[:n_rows]
        acc[1] = both[n_rows:]

    def mine(way, h):
        return acc[way, :, h * sub : (h + 1) * sub]

    far = sums([(z + hops) % nz])
    rs_send(0, 0, 0, far[:, :sub])
    rs_send(1, 1, 0, far[:, sub:])
    fill(1)
    rs_send(0, 1, 1, mine(0, 1))
    rs_send(1, 0, 1, mine(1, 0))
    rs_send(0, 0, 1, mine(0, 0) + rs_got(0, 0, 0))
    rs_send(1, 1, 1, mine(1, 1) + rs_got(1, 1, 0))
    fill(2)

    def rs_step(s, carry):
        for h in range(2):
            for way in range(2):
                rs_send(way, h, s, mine(way, h) + rs_got(way, h, s - 1))
        fill(s + 1)
        return carry

    lax.fori_loop(2, hops, rs_step, 0)
    last = hops - 1
    own = jnp.concatenate(
        [mine(0, h) + rs_got(0, h, last) + rs_got(1, h, last) for h in range(2)], axis=1
    )

    own_cols[...] = own.astype(jnp.bfloat16).reshape(ny, cl, kq)
    order = own.reshape(ny, nx, 2, 8, kq)
    rows[0] = jnp.concatenate(
        [order[yy, xx, cc] for cc in range(2) for xx in range(nx) for yy in range(ny)], axis=0
    ).astype(jnp.bfloat16)

    def c_copy(o):
        return remote(own_cols.at[(y + o) % ny], cols.at[0, o], c_ss.at[o], c_rs.at[o], y_peer(o))

    def r_copy(o):
        return remote(rows.at[0], rows.at[o], r_ss.at[o], r_rs.at[o], y_peer(o))

    for o in range(1, ny):
        c_copy(o).start()
    for o in range(1, ny):
        r_copy(o).start()
    cols[0, 0] = own_cols[y]

    hq = ny // 2

    def g_copy(way, h, d):
        if way == 0:
            src, dst = (nz - d + 1) % nz, nz - d
        else:
            src, dst = d - 1, d
        return remote(
            cols.at[src, pl.ds(h * hq, hq)], cols.at[dst, pl.ds(h * hq, hq)],
            g_ss.at[way, h, d - 1], g_rs.at[way, h, d - 1], z_next[way],
        )

    for h in range(2):
        for o in range(max(1, h * hq), (h + 1) * hq):
            c_copy(o).wait_recv()
        for way in range(2):
            g_copy(way, h, 1).start()

    own_quer.wait()
    total = None
    for q in range(ny):
        at = pl.multiple_of(((y + ny - q) % ny) * kq, kq)
        term = lax.dot_general(
            cols[0, q], quer[:, pl.ds(at, kq)], (((1,), (1,)), ((), ())), preferred_element_type=jnp.float32
        )
        total = term if total is None else total + term
    total = total.reshape(nx, 2, 8, total.shape[1])
    for cc in range(2):
        for xx in range(nx):
            s_part[cc, xx] = total[xx, cc]

    def sp_copy():
        return remote(s_part.at[1 - core], s_pair_in, sp_ss.at[0], sp_rs.at[0], mate)

    def sx_copy(o):
        return remote(s_half.at[(x + o) % nx], s_x_in.at[o], sx_ss.at[o], sx_rs.at[o], x_peer(o))

    sp_copy().start()
    for o in range(1, ny):
        r_copy(o).wait_recv()

    def block(d, g):
        first = (d % 2) * (d - 1) + (1 - d % 2) * (nz - d)
        total = None
        for q in range(ny):
            pair = cols[pl.ds(first, 2), q].reshape(2 * cl, kq)
            term = lax.dot_general(
                rows[q], pair, (((1,), (1,)), ((), ())), preferred_element_type=jnp.float32
            )
            total = term if total is None else total + term
        part[g] = total.reshape(2, nx, ny, 8, 2 * cl)

    def p_copy(g):
        return remote(part.at[g, 1 - core], pair_in.at[g], p_ss.at[g], p_rs.at[g], mate)

    def x_copy(g, o):
        return remote(half.at[g, (x + o) % nx], x_in.at[g, o], x_ss.at[g, o], x_rs.at[g, o], x_peer(o))

    def pair_sum(g):
        p_copy(g).wait_recv()
        half[g] = part[g, core] + pair_in[g]
        for o in range(1, nx):
            x_copy(g, o).start()

    def x_sum(g):
        d = g + 1
        first = (d % 2) * (d - 1) + (1 - d % 2) * (nz - d)
        total = half[g, x]
        for o in range(1, nx):
            x_copy(g, o).wait_recv()
            total = total + x_in[g, o]
        at = first // 2
        for yy in range(ny):
            done[yy, at] = total[yy]

    def gather_step(d, carry):
        for h in range(2):
            for way in range(2):
                g_copy(way, h, d).wait_recv()
                g_copy(way, h, d + 1).start()
        block(d, d - 1)
        p_copy(d - 1).start()

        @pl.when(d >= 2)
        def _():
            pair_sum(d - 2)

        @pl.when(d >= 3)
        def _():
            x_sum(d - 3)

        return carry

    lax.fori_loop(1, hops - 1, gather_step, 0)
    d = hops - 1
    for h in range(2):
        for way in range(2):
            g_copy(way, h, d).wait_recv()
            if way == h:
                g_copy(way, h, d + 1).start()
    block(d, d - 1)
    p_copy(d - 1).start()
    pair_sum(d - 2)
    x_sum(d - 3)
    sp_copy().wait_recv()
    s_half[...] = s_part[core] + s_pair_in[...]
    for o in range(1, nx):
        sx_copy(o).start()
    d = hops
    for h in range(2):
        g_copy(h, h, d).wait_recv()
    block(d, d - 1)
    p_copy(d - 1).start()
    pair_sum(d - 2)
    x_sum(d - 3)
    total = s_half[x]
    for o in range(1, nx):
        sx_copy(o).wait_recv()
        total = total + s_x_in[o]
    scores_ref[...] = total * ((kd * dims) ** -0.5)
    pair_sum(d - 1)
    x_sum(d - 2)
    x_sum(d - 1)

    def f_copy(o):
        return remote(done.at[(y + o) % ny], y_in.at[o], f_ss.at[o], f_rs.at[o], y_peer(o))

    for o in range(1, ny):
        f_copy(o).start()
    width = nz * cl
    for o in range(ny):
        if o:
            f_copy(o).wait_recv()
            got = y_in[o]
        else:
            got = done[y]
        wide = jnp.concatenate([got[g] for g in range(groups)], axis=1) * (1.0 / (kd * dims))
        at = pl.multiple_of(((y + ny - o) % ny) * width, width)
        gram_ref[:, pl.ds(at, width)] = pltpu.roll(wide, z * cl, 1)

    for o in range(1, ny):
        ids_copy(o).wait_send()
        for h in range(2):
            docs_copy(o, h).wait_send()
        c_copy(o).wait_send()
        r_copy(o).wait_send()
        f_copy(o).wait_send()
    sp_copy().wait_send()
    for o in range(1, nx):
        sx_copy(o).wait_send()
    rs_copy(0, 0, 0).wait_send()
    rs_copy(1, 1, 0).wait_send()
    g_copy(0, 0, hops).wait_send()
    g_copy(1, 1, hops).wait_send()

    def drain(s, carry):
        for way in range(2):
            for h in range(2):
                rs_copy(way, h, s).wait_send()
                g_copy(way, h, s).wait_send()
        return carry

    lax.fori_loop(1, hops, drain, 0)

    def drain_sums(g, carry):
        p_copy(g).wait_send()
        for o in range(1, nx):
            x_copy(g, o).wait_send()
        return carry

    lax.fori_loop(0, groups, drain_sums, 0)


def per_device(ny, cl, sketches, clusters, queries):
    nz = lax.axis_size("docs") // ny
    nx = lax.axis_size("dim") // 2
    n_docs, kd = sketches.shape
    nq = queries.shape[0]
    kq, rows, hops, groups = kd // ny, ny * cl, nz // 2, nz // 2
    ids = jnp.broadcast_to(clusters[None, :], (8, n_docs))
    f32, bf16, i32, i16 = jnp.float32, jnp.bfloat16, jnp.int32, jnp.int16
    vmem, dma = pltpu.VMEM, pltpu.SemaphoreType.DMA
    whole = pl.BlockSpec(memory_space=pltpu.VMEM)
    away = pl.BlockSpec(memory_space=pl.ANY)
    return pl.pallas_call(
        functools.partial(kernel, (ny, nz, nx, cl)),
        out_shape=(
            jax.ShapeDtypeStruct((8, ny * nz * cl), f32),
            jax.ShapeDtypeStruct((8, nq), f32),
        ),
        in_specs=[away, whole, away],
        out_specs=(whole, whole),
        scratch_shapes=[
            vmem((ny, n_docs, kq), bf16),
            vmem((ny, 8, n_docs), i32),
            vmem((nq, kd), bf16),
            vmem((ny, 8, n_docs), i32),
            vmem((ny, 8, n_docs), i32),
            vmem((2, rows, kq), f32),
            vmem((2, 2, hops, rows + 16, kq // 2), i16),
            vmem((2, 2, hops, rows + 16, kq // 2), i16),
            vmem((ny, cl, kq), bf16),
            vmem((nz, ny, cl, kq), bf16),
            vmem((ny, rows, kq), bf16),
            vmem((groups, 2, nx, ny, 8, 2 * cl), f32),
            vmem((groups, nx, ny, 8, 2 * cl), f32),
            vmem((groups, nx, ny, 8, 2 * cl), f32),
            vmem((groups, nx, ny, 8, 2 * cl), f32),
            vmem((ny, groups, 8, 2 * cl), f32),
            vmem((ny, groups, 8, 2 * cl), f32),
            vmem((2, nx, 8, nq), f32),
            vmem((nx, 8, nq), f32),
            vmem((nx, 8, nq), f32),
            vmem((nx, 8, nq), f32),
            dma((2,)),
            dma((ny, 2)), dma((ny, 2)),
            dma((ny,)), dma((ny,)),
            dma((2, 2, hops)), dma((2, 2, hops)),
            dma((ny,)), dma((ny,)),
            dma((ny,)), dma((ny,)),
            dma((2, 2, hops)), dma((2, 2, hops)),
            dma((groups,)), dma((groups,)),
            dma((groups, nx)), dma((groups, nx)),
            dma((ny,)), dma((ny,)),
            dma((1,)), dma((1,)),
            dma((nx,)), dma((nx,)),
        ],
        compiler_params=pltpu.CompilerParams(
            collective_id=0, has_side_effects=True, vmem_limit_bytes=56 * 1024 * 1024
        ),
    )(sketches, ids, queries)


def solution(mesh, ny=NY, cl=CL):
    in_specs = (P("docs", "dim"), P("docs"), P(None, "dim"))
    out_specs = (P(("docs", "dim"), None), P(("docs", "dim"), None))
    return jax.shard_map(
        functools.partial(per_device, ny, cl), mesh=mesh, in_specs=in_specs, out_specs=out_specs, check_vma=False
    )
```

```python
import functools
import math

import jax
import jax.numpy as jnp
from jax import lax
from jax.experimental import pallas as pl
from jax.experimental.pallas import tpu as pltpu
from jax.sharding import PartitionSpec as P

MESH = pl.DeviceIdType.MESH
CL = 64
NY = 4
LN2 = math.log(2.0)
BITS = 15


def power(level):
    return jnp.exp(level * LN2).astype(jnp.bfloat16).astype(jnp.float32)


def quantise(part):
    peak = jnp.maximum(jnp.max(jnp.abs(part), axis=0, keepdims=True), 1e-30)
    level = jnp.floor(jnp.log(peak) * (1.0 / LN2) + 0.001) + 1.0
    values = jnp.round(part * power(BITS - level)).astype(jnp.int32).astype(jnp.int16)
    levels = jnp.broadcast_to(level, (16, part.shape[1])).astype(jnp.int32).astype(jnp.int16)
    return values, levels


def restore(values, levels):
    level = levels.astype(jnp.int32).astype(jnp.float32)[0:1]
    return values.astype(jnp.int32).astype(jnp.float32) * power(level - BITS)


def kernel(
    sizes, sk_ref, ids_ref, qu_ref, gram_ref, scores_ref,
    docs_in, ids_in, quer, zpos, row, far, acc, rs_out, rs_in, own_cols, cols, rows,
    part, pair_in, half, x_in, done, packed, y_in, s_part, s_pair_in, s_half, s_x_in,
    local_sem, a_ss, a_rs, i_ss, i_rs, rs_ss, rs_rs, c_ss, c_rs, r_ss, r_rs, g_ss, g_rs,
    p_ss, p_rs, x_ss, x_rs, f_ss, f_rs, sp_ss, sp_rs, sx_ss, sx_rs,
):
    ny, nz, nx, cl = sizes
    n_docs, kd = sk_ref.shape
    members = 2 * ny
    kq = kd // members
    pairs = nz // 2
    n_rows = members * cl // 2
    hops = pairs // 2
    groups = pairs // 2
    dims = 2 * nx

    docs_at = lax.axis_index("docs")
    dim_at = lax.axis_index("dim")
    y, z = docs_at // nz, docs_at % nz
    zz, zp = z // 2, z % 2
    x, core = dim_at // 2, dim_at % 2

    def dev(yy, zz, zp, xx, cc):
        return (yy * nz + zz * 2 + zp, xx * 2 + cc)

    def member(o):
        return ((y + o // 2) % ny) * 2 + (zp + o % 2) % 2

    def member_from(o):
        return ((y + ny - o // 2) % ny) * 2 + (zp + o % 2) % 2

    def peer(o):
        return dev((y + o // 2) % ny, zz, (zp + o % 2) % 2, x, core)

    def x_peer(o):
        return dev(y, zz, zp, (x + o) % nx, core)

    z_next = (dev(y, (zz + 1) % pairs, zp, x, core), dev(y, (zz + pairs - 1) % pairs, zp, x, core))
    mate = dev(y, zz, zp, x, 1 - core)

    def remote(src, dst, ssem, rsem, to):
        return pltpu.make_async_remote_copy(
            src_ref=src, dst_ref=dst, send_sem=ssem, recv_sem=rsem, device_id=to, device_id_type=MESH
        )

    own_docs = pltpu.make_async_copy(
        sk_ref.at[:, pl.ds(pl.multiple_of(member(0) * kq, kq), kq)], docs_in.at[0], local_sem.at[0]
    )
    own_docs.start()

    barrier = pltpu.get_barrier_semaphore()
    partners = [peer(o) for o in range(1, members)] + [x_peer(o) for o in range(1, nx)] + list(z_next) + [mate]
    for to in partners:
        pl.semaphore_signal(barrier, inc=1, device_id=to, device_id_type=MESH)
    pl.semaphore_wait(barrier, len(partners))

    def ids_copy(o):
        return remote(ids_ref, ids_in.at[o], i_ss.at[o], i_rs.at[o], peer(o))

    def docs_copy(o):
        at = pl.multiple_of(member(o) * kq, kq)
        return remote(sk_ref.at[:, pl.ds(at, kq)], docs_in.at[o], a_ss.at[o], a_rs.at[o], peer(o))

    for o in range(1, members):
        ids_copy(o).start()
    for o in range(1, members):
        docs_copy(o).start()
    own_quer = pltpu.make_async_copy(qu_ref, quer, local_sem.at[1])
    own_quer.start()
    ids_in[0] = ids_ref[...]

    def place(o):
        ids = ids_in[o]
        owner = lax.shift_right_logical(ids, int(math.log2(cl)))
        local = lax.bitwise_and(ids, cl - 1)
        zpos[o] = lax.bitwise_and(lax.shift_right_logical(owner, 1), pairs - 1)
        who = lax.shift_right_logical(owner, int(math.log2(nz))) * 2 + lax.bitwise_and(owner, 1)
        upper = lax.shift_right_logical(local, int(math.log2(cl // 2)))
        row[o] = upper * n_rows + who * (cl // 2) + lax.bitwise_and(local, cl // 2 - 1)

    def onehot(o, target):
        places = lax.broadcasted_iota(jnp.int32, (2 * n_rows, n_docs), 0)
        here = jnp.where(zpos[o, 0:1, :] == target, row[o, 0:1, :], -1)
        return (here == places).astype(jnp.float32).astype(jnp.bfloat16)

    def sums(target):
        hot = jnp.concatenate([onehot(o, target) for o in range(members)], axis=1)
        return jnp.dot(hot, docs_in[...].reshape(members * n_docs, kq), preferred_element_type=jnp.float32)

    def rs_copy(way, h, s):
        return remote(
            rs_out.at[way, h, s], rs_in.at[way, h, s], rs_ss.at[way, h, s], rs_rs.at[way, h, s], z_next[way]
        )

    def rs_send(way, h, s, value):
        values, levels = quantise(value)
        rs_out[way, h, s, 0:n_rows] = values
        rs_out[way, h, s, n_rows : n_rows + 16] = levels
        rs_copy(way, h, s).start()

    def rs_got(way, h, s):
        rs_copy(way, h, s).wait_recv()
        return restore(rs_in[way, h, s, 0:n_rows], rs_in[way, h, s, n_rows : n_rows + 16])

    def mine(way, h):
        return acc[way, h * n_rows : (h + 1) * n_rows]

    first = [(zz + hops) % pairs, (zz + hops - 1) % pairs, (zz + pairs - hops + 1) % pairs]
    for o in range(members):
        if o:
            ids_copy(o).wait_recv()
            place(o)
            docs_copy(o).wait_recv()
        else:
            place(o)
            own_docs.wait()
        hot = jnp.concatenate([onehot(o, t) for t in first], axis=0)
        terms = jnp.dot(hot, docs_in[o], preferred_element_type=jnp.float32)
        for n, ref in enumerate((far, acc.at[0], acc.at[1])):
            term = terms[n * 2 * n_rows : (n + 1) * 2 * n_rows]
            ref[...] = term if o == 0 else ref[...] + term

    for s in range(hops):
        for h in range(2):
            for way in range(2):
                if s == 0:
                    if way == h:
                        rs_send(way, h, s, far[h * n_rows : (h + 1) * n_rows])
                elif s == 1 and way != h:
                    rs_send(way, h, s, mine(way, h))
                else:
                    rs_send(way, h, s, mine(way, h) + rs_got(way, h, s - 1))
        if s == 0:
            pass
        elif s + 1 < hops:
            acc[0] = sums((zz + hops - s - 1) % pairs)
            acc[1] = sums((zz + pairs - hops + s + 1) % pairs)
        else:
            acc[0] = sums(zz)

    def c_copy(h, o):
        return remote(own_cols.at[h, member(o)], cols.at[0, h, o], c_ss.at[h, o], c_rs.at[h, o], peer(o))

    def g_copy(way, h, d):
        if way == 0:
            src, dst = (pairs - d + 1) % pairs, pairs - d
        else:
            src, dst = d - 1, d
        return remote(
            cols.at[src, h], cols.at[dst, h], g_ss.at[way, h, d - 1], g_rs.at[way, h, d - 1], z_next[way]
        )

    own = []
    for h in range(2):
        own.append(mine(0, h) + rs_got(0, h, hops - 1) + rs_got(1, h, hops - 1))
        own_cols[h] = own[h].astype(jnp.bfloat16).reshape(members, cl // 2, kq)
        for o in range(1, members):
            c_copy(h, o).start()
        cols[0, h, 0] = own_cols[h, member(0)]
    order = [value.reshape(members, nx, 8, kq) for value in own]
    rows[0] = jnp.concatenate(
        [
            order[(2 * xx + cc) // nx][m, (2 * xx + cc) % nx]
            for cc in range(2) for xx in range(nx) for m in range(members)
        ],
        axis=0,
    ).astype(jnp.bfloat16)

    def r_copy(o):
        if o == 1:
            return remote(rows.at[0], rows.at[1], r_ss.at[1], r_rs.at[1], peer(1))
        return remote(rows.at[o % 2], rows.at[o], r_ss.at[o], r_rs.at[o], peer(o - o % 2))

    r_copy(1).start()
    for o in range(2, members, 2):
        r_copy(o).start()

    for h in range(2):
        for o in range(1, members):
            c_copy(h, o).wait_recv()
        for way in range(2):
            g_copy(way, h, 1).start()

    own_quer.wait()

    def wide(at):
        return jnp.concatenate(
            [jnp.concatenate([cols[at, h, o] for o in range(members)], axis=1) for h in range(2)], axis=0
        )

    asked = jnp.concatenate(
        [quer[:, pl.ds(pl.multiple_of(member_from(o) * kq, kq), kq)] for o in range(members)], axis=1
    )
    total = lax.dot_general(wide(0), asked, (((1,), (1,)), ((), ())), preferred_element_type=jnp.float32)
    total = total.reshape(nx, 2, 8, total.shape[1])
    for cc in range(2):
        for xx in range(nx):
            s_part[cc, xx] = total[xx, cc]

    def sp_copy():
        return remote(s_part.at[1 - core], s_pair_in, sp_ss.at[0], sp_rs.at[0], mate)

    def sx_copy(o):
        return remote(s_half.at[(x + o) % nx], s_x_in.at[o], sx_ss.at[o], sx_rs.at[o], x_peer(o))

    sp_copy().start()
    r_copy(1).wait_recv()
    for o in range(3, members, 2):
        r_copy(o).start()

    def block(g, low, high):
        these = jnp.concatenate([rows[o] for o in range(members)], axis=1)
        those = jnp.concatenate([wide(low), wide(high)], axis=0)
        total = lax.dot_general(these, those, (((1,), (1,)), ((), ())), preferred_element_type=jnp.float32)
        part[g] = total.reshape(2, nx, members, 8, 2 * cl)
        p_copy(g).start()

    def p_copy(g):
        return remote(part.at[g, 1 - core], pair_in.at[g], p_ss.at[g], p_rs.at[g], mate)

    def x_copy(g, o):
        return remote(half.at[g, (x + o) % nx], x_in.at[g, o], x_ss.at[g, o], x_rs.at[g, o], x_peer(o))

    def pair_sum(g):
        p_copy(g).wait_recv()
        half[g] = part[g, core] + pair_in[g]
        for o in range(1, nx):
            x_copy(g, o).start()

    def x_sum(g, low, high):
        total = half[g, x]
        for o in range(1, nx):
            x_copy(g, o).wait_recv()
            total = total + x_in[g, o]
        turned = pltpu.roll(total.reshape(members * 8, 2 * cl), cl, 1).reshape(total.shape)
        for m in range(members):
            done[m, (zz + low) % pairs] = total[m]
            done[m, (zz + high) % pairs] = turned[m]

    spots = [(pairs - d, d) for d in range(1, hops)] + [(0, hops)]
    for d in range(1, hops + 1):
        for h in range(2):
            for way in range(2):
                if d < hops or way == h:
                    g_copy(way, h, d).wait_recv()
                    if d + 1 < hops or (d + 1 == hops and way == h):
                        g_copy(way, h, d + 1).start()
        if d == 1:
            sp_copy().wait_recv()
            s_half[...] = s_part[core] + s_pair_in[...]
            for o in range(1, nx):
                sx_copy(o).start()
            for o in range(2, members):
                r_copy(o).wait_recv()
        block(d - 1, *spots[d - 1])
        if d >= 2:
            pair_sum(d - 2)
        if d >= 3:
            x_sum(d - 3, *spots[d - 3])
    total = s_half[x]
    for o in range(1, nx):
        sx_copy(o).wait_recv()
        total = total + s_x_in[o]
    scores_ref[...] = total * ((kd * dims) ** -0.5)
    if hops >= 2:
        x_sum(hops - 2, *spots[hops - 2])
    pair_sum(hops - 1)
    x_sum(hops - 1, *spots[hops - 1])

    lower = lax.broadcasted_iota(jnp.int32, (8, 2 * cl), 1) < cl
    for m in range(members):
        for t in range(pairs // 2):
            packed[m, t] = jnp.where(lower, done[m, 2 * t], pltpu.roll(done[m, 2 * t + 1], cl, 1))

    def f_copy(o):
        return remote(packed.at[member(o)], y_in.at[o], f_ss.at[o], f_rs.at[o], peer(o))

    for o in range(1, members):
        f_copy(o).start()
    y_in[0] = packed[member(0)]
    scale = 1.0 / (kd * dims)
    width = nz * cl
    for o in range(0, members, 2):
        for p in range(2):
            if o + p:
                f_copy(o + p).wait_recv()
        same, other = y_in[o], y_in[o + 1]
        even = jnp.where(zp == 0, same, other) * scale
        odd = jnp.where(zp == 0, other, same) * scale
        tiles = []
        for t in range(pairs // 2):
            tiles.append(jnp.where(lower, even[t], pltpu.roll(odd[t], cl, 1)))
            tiles.append(jnp.where(lower, pltpu.roll(even[t], cl, 1), odd[t]))
        at = pl.multiple_of(((y + ny - o // 2) % ny) * width, width)
        gram_ref[:, pl.ds(at, width)] = jnp.concatenate(tiles, axis=1)

    for o in range(1, members):
        ids_copy(o).wait_send()
        docs_copy(o).wait_send()
        for h in range(2):
            c_copy(h, o).wait_send()
        r_copy(o).wait_send()
        f_copy(o).wait_send()
    sp_copy().wait_send()
    for o in range(1, nx):
        sx_copy(o).wait_send()
    for s in range(hops):
        for way in range(2):
            for h in range(2):
                if s or way == h:
                    rs_copy(way, h, s).wait_send()
                if s + 1 < hops or way == h:
                    g_copy(way, h, s + 1).wait_send()
    for g in range(groups):
        p_copy(g).wait_send()
        for o in range(1, nx):
            x_copy(g, o).wait_send()


def per_device(ny, cl, sketches, clusters, queries):
    nz = lax.axis_size("docs") // ny
    nx = lax.axis_size("dim") // 2
    n_docs, kd = sketches.shape
    nq = queries.shape[0]
    members, pairs = 2 * ny, nz // 2
    kq, rows, hops, groups = kd // members, members * cl, pairs // 2, pairs // 2
    ids = clusters.reshape(1, n_docs)
    f32, bf16, i32, i16 = jnp.float32, jnp.bfloat16, jnp.int32, jnp.int16
    vmem, dma = pltpu.VMEM, pltpu.SemaphoreType.DMA
    whole = pl.BlockSpec(memory_space=pltpu.VMEM)
    away = pl.BlockSpec(memory_space=pl.ANY)
    return pl.pallas_call(
        functools.partial(kernel, (ny, nz, nx, cl)),
        out_shape=(
            jax.ShapeDtypeStruct((8, ny * nz * cl), f32),
            jax.ShapeDtypeStruct((8, nq), f32),
        ),
        in_specs=[away, whole, away],
        out_specs=(whole, whole),
        scratch_shapes=[
            vmem((members, n_docs, kq), bf16),
            vmem((members, 1, n_docs), i32),
            vmem((nq, kd), bf16),
            vmem((members, 1, n_docs), i32),
            vmem((members, 1, n_docs), i32),
            vmem((rows, kq), f32),
            vmem((2, rows, kq), f32),
            vmem((2, 2, hops, rows // 2 + 16, kq), i16),
            vmem((2, 2, hops, rows // 2 + 16, kq), i16),
            vmem((2, members, cl // 2, kq), bf16),
            vmem((pairs, 2, members, cl // 2, kq), bf16),
            vmem((members, rows, kq), bf16),
            vmem((groups, 2, nx, members, 8, 2 * cl), f32),
            vmem((groups, nx, members, 8, 2 * cl), f32),
            vmem((groups, nx, members, 8, 2 * cl), f32),
            vmem((groups, nx, members, 8, 2 * cl), f32),
            vmem((members, pairs, 8, 2 * cl), f32),
            vmem((members, pairs // 2, 8, 2 * cl), f32),
            vmem((members, pairs // 2, 8, 2 * cl), f32),
            vmem((2, nx, 8, nq), f32),
            vmem((nx, 8, nq), f32),
            vmem((nx, 8, nq), f32),
            vmem((nx, 8, nq), f32),
            dma((2,)),
            dma((members,)), dma((members,)),
            dma((members,)), dma((members,)),
            dma((2, 2, hops)), dma((2, 2, hops)),
            dma((2, members)), dma((2, members)),
            dma((members,)), dma((members,)),
            dma((2, 2, hops)), dma((2, 2, hops)),
            dma((groups,)), dma((groups,)),
            dma((groups, nx)), dma((groups, nx)),
            dma((members,)), dma((members,)),
            dma((1,)), dma((1,)),
            dma((nx,)), dma((nx,)),
        ],
        compiler_params=pltpu.CompilerParams(
            collective_id=0, has_side_effects=True, vmem_limit_bytes=56 * 1024 * 1024
        ),
    )(sketches, ids, queries)


def solution(mesh, ny=NY, cl=CL):
    in_specs = (P("docs", "dim"), P("docs"), P(None, "dim"))
    out_specs = (P(("docs", "dim"), None), P(("docs", "dim"), None))
    return jax.shard_map(
        functools.partial(per_device, ny, cl), mesh=mesh, in_specs=in_specs, out_specs=out_specs, check_vma=False
    )
```

```python
import functools
import math

import jax
import jax.numpy as jnp
from jax import lax
from jax.experimental import pallas as pl
from jax.experimental.pallas import tpu as pltpu
from jax.sharding import PartitionSpec as P

MESH = pl.DeviceIdType.MESH
CL = 64
NY = 4
LN2 = math.log(2.0)
BITS = 15


def power(level):
    return jnp.exp(level * LN2).astype(jnp.bfloat16).astype(jnp.float32)


def quantise(part):
    peak = jnp.maximum(jnp.max(jnp.abs(part), axis=0, keepdims=True), 1e-30)
    level = jnp.floor(jnp.log(peak) * (1.0 / LN2) + 0.001) + 1.0
    values = jnp.round(part * power(BITS - level)).astype(jnp.int32).astype(jnp.int16)
    levels = jnp.broadcast_to(level, (16, part.shape[1])).astype(jnp.int32).astype(jnp.int16)
    return values, levels


def restore(values, levels):
    level = levels.astype(jnp.int32).astype(jnp.float32)[0:1]
    return values.astype(jnp.int32).astype(jnp.float32) * power(level - BITS)


def kernel(
    sizes, sk_ref, ids_ref, qu_ref, gram_ref, scores_ref,
    docs_in, ids_in, quer, zpos, row, far, acc, rs_out, rs_in, own_cols, cols, rows,
    part, pair_in, half, x_in, done, f_in, e_part, e_pair_in, e_half, e_x_in, e_done, e_f_in,
    s_part, s_pair_in, s_half, s_x_in,
    local_sem, a_ss, a_rs, i_ss, i_rs, rs_ss, rs_rs, c_ss, c_rs, r_ss, r_rs, g_ss, g_rs,
    p_ss, p_rs, x_ss, x_rs, f_ss, f_rs, sp_ss, sp_rs, sx_ss, sx_rs,
):
    ny, nz, nx, cl = sizes
    n_docs, kd = sk_ref.shape
    members = 2 * ny
    kq = kd // members
    pairs = nz // 2
    n_rows = members * cl // 2
    hops = pairs // 2
    last = hops - 1
    dims = 2 * nx

    docs_at = lax.axis_index("docs")
    dim_at = lax.axis_index("dim")
    y, z = docs_at // nz, docs_at % nz
    zz, zp = z // 2, z % 2
    x, core = dim_at // 2, dim_at % 2

    def dev(yy, zz, zp, xx, cc):
        return (yy * nz + zz * 2 + zp, xx * 2 + cc)

    def member(o):
        return ((y + o // 2) % ny) * 2 + (zp + o % 2) % 2

    def member_from(o):
        return ((y + ny - o // 2) % ny) * 2 + (zp + o % 2) % 2

    def peer(o):
        return dev((y + o // 2) % ny, zz, (zp + o % 2) % 2, x, core)

    def x_peer(o):
        return dev(y, zz, zp, (x + o) % nx, core)

    z_next = (dev(y, (zz + 1) % pairs, zp, x, core), dev(y, (zz + pairs - 1) % pairs, zp, x, core))
    mate = dev(y, zz, zp, x, 1 - core)

    def remote(src, dst, ssem, rsem, to):
        return pltpu.make_async_remote_copy(
            src_ref=src, dst_ref=dst, send_sem=ssem, recv_sem=rsem, device_id=to, device_id_type=MESH
        )

    own_docs = pltpu.make_async_copy(
        sk_ref.at[:, pl.ds(pl.multiple_of(member(0) * kq, kq), kq)], docs_in.at[0], local_sem.at[0]
    )
    own_docs.start()
    own_ids = pltpu.make_async_copy(ids_ref, ids_in.at[0], local_sem.at[2])
    own_ids.start()

    barrier = pltpu.get_barrier_semaphore()
    partners = [peer(o) for o in range(1, members)] + [x_peer(o) for o in range(1, nx)] + list(z_next) + [mate]
    for to in partners:
        pl.semaphore_signal(barrier, inc=1, device_id=to, device_id_type=MESH)
    pl.semaphore_wait(barrier, len(partners))

    def ids_copy(o):
        return remote(ids_ref, ids_in.at[o], i_ss.at[o], i_rs.at[o], peer(o))

    def docs_copy(o):
        at = pl.multiple_of(member(o) * kq, kq)
        return remote(sk_ref.at[:, pl.ds(at, kq)], docs_in.at[o], a_ss.at[o], a_rs.at[o], peer(o))

    for o in range(1, members):
        ids_copy(o).start()
    for o in range(1, members):
        docs_copy(o).start()
    own_quer = pltpu.make_async_copy(qu_ref, quer, local_sem.at[1])
    own_quer.start()

    def place(o):
        ids = ids_in[o]
        owner = lax.shift_right_logical(ids, int(math.log2(cl)))
        local = lax.bitwise_and(ids, cl - 1)
        zpos[o] = lax.bitwise_and(lax.shift_right_logical(owner, 1), pairs - 1)
        who = lax.shift_right_logical(owner, int(math.log2(nz))) * 2 + lax.bitwise_and(owner, 1)
        upper = lax.shift_right_logical(local, int(math.log2(cl // 2)))
        row[o] = upper * n_rows + who * (cl // 2) + lax.bitwise_and(local, cl // 2 - 1)

    def onehot(o, target):
        places = lax.broadcasted_iota(jnp.int32, (2 * n_rows, n_docs), 0)
        here = jnp.where(zpos[o, 0:1, :] == target, row[o, 0:1, :], -1)
        return (here == places).astype(jnp.float32).astype(jnp.bfloat16)

    def sums(target):
        hot = jnp.concatenate([onehot(o, target) for o in range(members)], axis=1)
        return jnp.dot(hot, docs_in[...].reshape(members * n_docs, kq), preferred_element_type=jnp.float32)

    def rs_copy(way, h, s):
        return remote(
            rs_out.at[way, h, s], rs_in.at[way, h, s], rs_ss.at[way, h, s], rs_rs.at[way, h, s], z_next[way]
        )

    def rs_send(way, h, s, value):
        values, levels = quantise(value)
        rs_out[way, h, s, 0:n_rows] = values
        rs_out[way, h, s, n_rows : n_rows + 16] = levels
        rs_copy(way, h, s).start()

    def rs_got(way, h, s):
        rs_copy(way, h, s).wait_recv()
        return restore(rs_in[way, h, s, 0:n_rows], rs_in[way, h, s, n_rows : n_rows + 16])

    def mine(way, h):
        return acc[way, h * n_rows : (h + 1) * n_rows]

    first = [(zz + hops) % pairs, (zz + hops - 1) % pairs, (zz + pairs - hops + 1) % pairs]
    def arrived(o):
        if o:
            ids_copy(o).wait_recv()
            place(o)
            docs_copy(o).wait_recv()
        else:
            own_ids.wait()
            place(o)
            own_docs.wait()

    near = sorted(range(members), key=lambda o: (min(o // 2, ny - o // 2), o % 2))
    for o in near[:-1]:
        arrived(o)
        hot = jnp.concatenate([onehot(o, t) for t in first], axis=0)
        terms = jnp.dot(hot, docs_in[o], preferred_element_type=jnp.float32)
        for n, ref in enumerate((far, acc.at[0], acc.at[1])):
            term = terms[n * 2 * n_rows : (n + 1) * 2 * n_rows]
            ref[...] = term if o == near[0] else ref[...] + term
    o = near[-1]
    arrived(o)
    term = far[...] + jnp.dot(onehot(o, first[0]), docs_in[o], preferred_element_type=jnp.float32)
    rs_send(0, 0, 0, term[:n_rows])
    rs_send(1, 1, 0, term[n_rows:])
    for n in range(2):
        acc[n] += jnp.dot(onehot(o, first[n + 1]), docs_in[o], preferred_element_type=jnp.float32)

    for s in range(1, hops):
        for h in range(2):
            for way in range(2):
                if s == 1 and way != h:
                    rs_send(way, h, s, mine(way, h))
        for h in range(2):
            for way in range(2):
                if s > 1 or way == h:
                    rs_send(way, h, s, mine(way, h) + rs_got(way, h, s - 1))
        if s + 1 < hops:
            acc[0] = sums((zz + hops - s - 1) % pairs)
            acc[1] = sums((zz + pairs - hops + s + 1) % pairs)
        else:
            acc[0] = sums(zz)

    def c_copy(h, o):
        return remote(own_cols.at[h, member(o)], cols.at[0, h, o], c_ss.at[h, o], c_rs.at[h, o], peer(o))

    quarter = members // 2

    def g_copy(way, e, d):
        if way == 0:
            src, dst = (pairs - d + 1) % pairs, pairs - d
        else:
            src, dst = d - 1, d
        h, those = e // 2, pl.ds(e % 2 * quarter, quarter)
        return remote(
            cols.at[src, h, those], cols.at[dst, h, those],
            g_ss.at[way, e, d - 1], g_rs.at[way, e, d - 1], z_next[way],
        )

    own = []
    for h in range(2):
        own.append(mine(0, h) + rs_got(0, h, hops - 1) + rs_got(1, h, hops - 1))
        own_cols[h] = own[h].astype(jnp.bfloat16).reshape(members, cl // 2, kq)
        for o in range(1, members):
            c_copy(h, o).start()
        cols[0, h, 0] = own_cols[h, member(0)]
    order = [value.reshape(members, nx, 8, kq) for value in own]
    rows[0] = jnp.concatenate(
        [
            order[(2 * xx + cc) // nx][m, (2 * xx + cc) % nx]
            for cc in range(2) for xx in range(nx) for m in range(members)
        ],
        axis=0,
    ).astype(jnp.bfloat16)

    def r_copy(o):
        if o == 1:
            return remote(rows.at[0], rows.at[1], r_ss.at[1], r_rs.at[1], peer(1))
        return remote(rows.at[o % 2], rows.at[o], r_ss.at[o], r_rs.at[o], peer(o - o % 2))

    r_copy(1).start()
    for o in range(2, members, 2):
        r_copy(o).start()

    for e in range(4):
        for o in range(max(1, e % 2 * quarter), (e % 2 + 1) * quarter):
            c_copy(e // 2, o).wait_recv()
        for way in range(2):
            g_copy(way, e, 1).start()

    def sp_copy():
        return remote(s_part.at[1 - core], s_pair_in, sp_ss.at[0], sp_rs.at[0], mate)

    def sx_copy(o):
        return remote(s_half.at[(x + o) % nx], s_x_in.at[o], sx_ss.at[o], sx_rs.at[o], x_peer(o))

    r_copy(1).wait_recv()
    for o in range(3, members, 2):
        r_copy(o).start()

    own_quer.wait()

    def wide(at):
        return jnp.concatenate(
            [jnp.concatenate([cols[at, h, o] for o in range(members)], axis=1) for h in range(2)], axis=0
        )

    asked = jnp.concatenate(
        [quer[:, pl.ds(pl.multiple_of(member_from(o) * kq, kq), kq)] for o in range(members)], axis=1
    )
    total = lax.dot_general(wide(0), asked, (((1,), (1,)), ((), ())), preferred_element_type=jnp.float32)
    total = total.reshape(nx, 2, 8, total.shape[1])
    for cc in range(2):
        for xx in range(nx):
            s_part[cc, xx] = total[xx, cc]
    sp_copy().start()

    lower = lax.broadcasted_iota(jnp.int32, (8, 2 * cl), 1) < cl

    def turn(tile):
        return pltpu.roll(tile, cl, 1)

    def p_copy(g):
        src, dst = (part.at[g], pair_in.at[g]) if g < last else (e_part.at[g - last], e_pair_in.at[g - last])
        return remote(src.at[1 - core], dst, p_ss.at[g], p_rs.at[g], mate)

    def x_copy(g, o):
        src, dst = (half.at[g], x_in.at[g]) if g < last else (e_half.at[g - last], e_x_in.at[g - last])
        return remote(src.at[(x + o) % nx], dst.at[o], x_ss.at[g, o], x_rs.at[g, o], x_peer(o))

    def f_copy(g, o):
        if g < last:
            src, dst = done.at[g, member(o)], f_in.at[g, o]
        else:
            src, dst = e_done.at[g - last, member(o) // 2], e_f_in.at[g - last, o]
        return remote(src, dst, f_ss.at[g, o], f_rs.at[g, o], peer(o))

    def block(g):
        these = jnp.concatenate([rows[o] for o in range(members)], axis=1)
        if g < last:
            those = jnp.concatenate([wide(pairs - g - 1), wide(g + 1)], axis=0)
        else:
            those = jnp.concatenate([wide((g - last) * hops)] * 2, axis=0)
        total = lax.dot_general(these, those, (((1,), (1,)), ((), ())), preferred_element_type=jnp.float32)
        total = total.reshape(2, nx, members, 8, 2 * cl)
        if g < last:
            part[g] = total
        else:
            two = total.reshape(2, nx, members // 2, 2, 8, 2 * cl)
            e_part[g - last] = jnp.where(lower, two[:, :, :, 0], two[:, :, :, 1])
        p_copy(g).start()

    def pair_sum(g):
        p_copy(g).wait_recv()
        if g < last:
            half[g] = part[g, core] + pair_in[g]
        else:
            e_half[g - last] = e_part[g - last, core] + e_pair_in[g - last]
        for o in range(1, nx):
            x_copy(g, o).start()

    def x_sum(g):
        mine, other = (half.at[g], x_in.at[g]) if g < last else (e_half.at[g - last], e_x_in.at[g - last])
        total = mine[x]
        for o in range(1, nx):
            x_copy(g, o).wait_recv()
            total = total + other[o]
        if g < last:
            done[g] = total
            f_in[g, 0] = done[g, member(0)]
        else:
            e_done[g - last] = total
            e_f_in[g - last, 0] = e_done[g - last, member(0) // 2]
        for o in range(1, members):
            f_copy(g, o).start()

    scale = 1.0 / (kd * dims)

    def store(at, tile):
        gram_ref[:, pl.ds(pl.multiple_of(at * 2 * cl, 2 * cl), 2 * cl)] = tile

    def finish(g):
        for o in range(1, members):
            f_copy(g, o).wait_recv()
        for o in range(0, members, 2):
            at = ((y + ny - o // 2) % ny) * pairs
            same, other = (f_in[g, o], f_in[g, o + 1]) if g < last else (e_f_in[g - last, o], e_f_in[g - last, o + 1])
            even = jnp.where(zp == 0, same, other) * scale
            odd = jnp.where(zp == 0, other, same) * scale
            left = jnp.where(lower, even, turn(odd))
            right = jnp.where(lower, turn(even), odd)
            if g < last:
                store(at + (zz + pairs - g - 1) % pairs, left)
                store(at + (zz + g + 1) % pairs, right)
            else:
                store(at + (zz + (g - last) * hops) % pairs, jnp.where(zp == 0, left, right))

    before, waiting = [], []
    for d in range(1, hops + 1):
        for e in range(4):
            for way in range(2):
                if d < hops or way == e // 2:
                    g_copy(way, e, d).wait_recv()
                    if d + 1 < hops or (d + 1 == hops and way == e // 2):
                        g_copy(way, e, d + 1).start()
        if d == 1:
            sp_copy().wait_recv()
            s_half[...] = s_part[core] + s_pair_in[...]
            for o in range(1, nx):
                sx_copy(o).start()
        if d == min(2, last):
            for o in range(2, members):
                r_copy(o).wait_recv()
            now = [last]
        else:
            now = []
        if 2 <= d < hops:
            now.append(d - 2)
        if d == last:
            now.append(last - 1)
        if d < hops:
            for g in waiting:
                pair_sum(g)
            for g in now:
                block(g)
            before, waiting = before + waiting, now
        if d == last:
            for g in waiting:
                pair_sum(g)
    block(hops)
    before = before + waiting
    for g in before[:-1]:
        x_sum(g)
    pair_sum(hops)
    x_sum(before[-1])
    total = s_half[x]
    for o in range(1, nx):
        sx_copy(o).wait_recv()
        total = total + s_x_in[o]
    scores_ref[...] = total * ((kd * dims) ** -0.5)
    x_sum(hops)
    for g in before + [hops]:
        finish(g)

    for o in range(1, members):
        ids_copy(o).wait_send()
        docs_copy(o).wait_send()
        for h in range(2):
            c_copy(h, o).wait_send()
        r_copy(o).wait_send()
    sp_copy().wait_send()
    for o in range(1, nx):
        sx_copy(o).wait_send()
    for s in range(hops):
        for way in range(2):
            for e in range(4):
                if e < 2 and (s or way == e):
                    rs_copy(way, e, s).wait_send()
                if s + 1 < hops or way == e // 2:
                    g_copy(way, e, s + 1).wait_send()
    for g in range(hops + 1):
        p_copy(g).wait_send()
        for o in range(1, nx):
            x_copy(g, o).wait_send()
        for o in range(1, members):
            f_copy(g, o).wait_send()


def hand_over(gram_in, scores_in, gram_ref, scores_ref):
    gram_ref[...] = gram_in[...]
    scores_ref[...] = scores_in[...]


def per_device(ny, cl, sketches, clusters, queries):
    nz = lax.axis_size("docs") // ny
    nx = lax.axis_size("dim") // 2
    n_docs, kd = sketches.shape
    nq = queries.shape[0]
    members, pairs = 2 * ny, nz // 2
    kq, rows, hops = kd // members, members * cl, pairs // 2
    last = hops - 1
    ids = clusters.reshape(1, n_docs)
    f32, bf16, i32, i16 = jnp.float32, jnp.bfloat16, jnp.int32, jnp.int16
    vmem, dma = pltpu.VMEM, pltpu.SemaphoreType.DMA
    whole = pl.BlockSpec(memory_space=pltpu.VMEM)
    away = pl.BlockSpec(memory_space=pl.ANY)
    gram, scores = pl.pallas_call(
        functools.partial(kernel, (ny, nz, nx, cl)),
        out_shape=(
            jax.ShapeDtypeStruct((8, ny * nz * cl), f32),
            jax.ShapeDtypeStruct((8, nq), f32),
        ),
        in_specs=[away, away, away],
        out_specs=(whole, whole),
        scratch_shapes=[
            vmem((members, n_docs, kq), bf16),
            vmem((members, 1, n_docs), i32),
            vmem((nq, kd), bf16),
            vmem((members, 1, n_docs), i32),
            vmem((members, 1, n_docs), i32),
            vmem((rows, kq), f32),
            vmem((2, rows, kq), f32),
            vmem((2, 2, hops, rows // 2 + 16, kq), i16),
            vmem((2, 2, hops, rows // 2 + 16, kq), i16),
            vmem((2, members, cl // 2, kq), bf16),
            vmem((pairs, 2, members, cl // 2, kq), bf16),
            vmem((members, rows, kq), bf16),
            vmem((last, 2, nx, members, 8, 2 * cl), f32),
            vmem((last, nx, members, 8, 2 * cl), f32),
            vmem((last, nx, members, 8, 2 * cl), f32),
            vmem((last, nx, members, 8, 2 * cl), f32),
            vmem((last, members, 8, 2 * cl), f32),
            vmem((last, members, 8, 2 * cl), f32),
            vmem((2, 2, nx, members // 2, 8, 2 * cl), f32),
            vmem((2, nx, members // 2, 8, 2 * cl), f32),
            vmem((2, nx, members // 2, 8, 2 * cl), f32),
            vmem((2, nx, members // 2, 8, 2 * cl), f32),
            vmem((2, members // 2, 8, 2 * cl), f32),
            vmem((2, members, 8, 2 * cl), f32),
            vmem((2, nx, 8, nq), f32),
            vmem((nx, 8, nq), f32),
            vmem((nx, 8, nq), f32),
            vmem((nx, 8, nq), f32),
            dma((3,)),
            dma((members,)), dma((members,)),
            dma((members,)), dma((members,)),
            dma((2, 2, hops)), dma((2, 2, hops)),
            dma((2, members)), dma((2, members)),
            dma((members,)), dma((members,)),
            dma((2, 4, hops)), dma((2, 4, hops)),
            dma((hops + 1,)), dma((hops + 1,)),
            dma((hops + 1, nx)), dma((hops + 1, nx)),
            dma((hops + 1, members)), dma((hops + 1, members)),
            dma((1,)), dma((1,)),
            dma((nx,)), dma((nx,)),
        ],
        compiler_params=pltpu.CompilerParams(
            collective_id=0, has_side_effects=True, vmem_limit_bytes=56 * 1024 * 1024
        ),
    )(sketches, ids, queries)
    return pl.pallas_call(
        hand_over,
        out_shape=(
            jax.ShapeDtypeStruct((8, ny * nz * cl), f32),
            jax.ShapeDtypeStruct((8, nq), f32),
        ),
        in_specs=[whole, whole],
        out_specs=(whole, whole),
    )(gram, scores)


def solution(mesh, ny=NY, cl=CL):
    in_specs = (P("docs", "dim"), P("docs"), P(None, "dim"))
    out_specs = (P(("docs", "dim"), None), P(("docs", "dim"), None))
    return jax.shard_map(
        functools.partial(per_device, ny, cl), mesh=mesh, in_specs=in_specs, out_specs=out_specs, check_vma=False
    )
```

```python
import functools
import math

import jax
import jax.numpy as jnp
from jax import lax
from jax.experimental import pallas as pl
from jax.experimental.pallas import tpu as pltpu
from jax.sharding import PartitionSpec as P

MESH = pl.DeviceIdType.MESH
CL = 64
NY = 4
LN2 = math.log(2.0)
BITS = 15
FINE = 16


def power(level):
    return jnp.exp(level * LN2).astype(jnp.bfloat16).astype(jnp.float32)


def peak(part):
    return jnp.maximum(jnp.max(jnp.abs(part), axis=0, keepdims=True), 1e-30)


def code(bound):
    return jnp.ceil(jnp.log(bound) * (FINE / LN2) + 0.01)


def bound_of(fine):
    return jnp.exp(fine * (LN2 / FINE))


def level_of(fine):
    return jnp.floor(fine * (1.0 / FINE)) + 1.0


def quantise(part, fine):
    return jnp.round(part * power(BITS - level_of(fine))).astype(jnp.int32).astype(jnp.int16)


def restore(values, fine):
    return values.astype(jnp.int32).astype(jnp.float32) * power(level_of(fine) - BITS)


def kernel(
    sizes, sk_ref, ids_ref, qu_ref, gram_ref, scores_ref,
    docs_in, ids_in, quer, zpos, row, far, acc, rs_out, rs_in, own_cols, cols, rows,
    part, pair_in, half, x_in, done, f_in, e_part, e_pair_in, e_half, e_x_in, e_done, e_f_in,
    s_part, s_pair_in, s_half, s_x_in,
    local_sem, a_ss, a_rs, i_ss, i_rs, rs_ss, rs_rs, c_ss, c_rs, r_ss, r_rs, g_ss, g_rs,
    p_ss, p_rs, x_ss, x_rs, f_ss, f_rs, sp_ss, sp_rs, sx_ss, sx_rs,
):
    ny, nz, nx, cl = sizes
    n_docs, kd = sk_ref.shape
    members = 2 * ny
    kq = kd // members
    pairs = nz // 2
    n_rows = members * cl // 2
    hops = pairs // 2
    last = hops - 1
    dims = 2 * nx

    docs_at = lax.axis_index("docs")
    dim_at = lax.axis_index("dim")
    y, z = docs_at // nz, docs_at % nz
    zz, zp = z // 2, z % 2
    x, core = dim_at // 2, dim_at % 2

    def dev(yy, zz, zp, xx, cc):
        return (yy * nz + zz * 2 + zp, xx * 2 + cc)

    def member(o):
        return ((y + o // 2) % ny) * 2 + (zp + o % 2) % 2

    def member_from(o):
        return ((y + ny - o // 2) % ny) * 2 + (zp + o % 2) % 2

    def peer(o):
        return dev((y + o // 2) % ny, zz, (zp + o % 2) % 2, x, core)

    def x_peer(o):
        return dev(y, zz, zp, (x + o) % nx, core)

    z_next = (dev(y, (zz + 1) % pairs, zp, x, core), dev(y, (zz + pairs - 1) % pairs, zp, x, core))
    mate = dev(y, zz, zp, x, 1 - core)

    def remote(src, dst, ssem, rsem, to):
        return pltpu.make_async_remote_copy(
            src_ref=src, dst_ref=dst, send_sem=ssem, recv_sem=rsem, device_id=to, device_id_type=MESH
        )

    def all_sent(ref, sem):
        remote(ref, ref, sem, local_sem.at[0], mate).wait_send()

    def all_got(ref, sem):
        remote(ref, ref, local_sem.at[0], sem, mate).wait_recv()

    own_docs = pltpu.make_async_copy(
        sk_ref.at[:, pl.ds(pl.multiple_of(member(0) * kq, kq), kq)], docs_in.at[0], local_sem.at[0]
    )
    own_docs.start()
    own_ids = pltpu.make_async_copy(ids_ref, ids_in.at[0], local_sem.at[2])
    own_ids.start()

    barrier = pltpu.get_barrier_semaphore()
    partners = [peer(o) for o in range(1, members)] + [x_peer(o) for o in range(1, nx)] + list(z_next) + [mate]
    for to in partners:
        pl.semaphore_signal(barrier, inc=1, device_id=to, device_id_type=MESH)
    pl.semaphore_wait(barrier, len(partners))

    def ids_copy(o):
        return remote(ids_ref, ids_in.at[o], i_ss.at[0], i_rs.at[0], peer(o))

    def docs_copy(o):
        at = pl.multiple_of(member(o) * kq, kq)
        return remote(sk_ref.at[:, pl.ds(at, kq)], docs_in.at[o], a_ss.at[0], a_rs.at[o], peer(o))

    for o in range(1, members):
        ids_copy(o).start()
    for o in range(1, members):
        docs_copy(o).start()
    own_quer = pltpu.make_async_copy(qu_ref, quer, local_sem.at[1])
    own_quer.start()

    def place(o):
        ids = ids_in[o]
        owner = lax.shift_right_logical(ids, int(math.log2(cl)))
        local = lax.bitwise_and(ids, cl - 1)
        zpos[o] = lax.bitwise_and(lax.shift_right_logical(owner, 1), pairs - 1)
        who = lax.shift_right_logical(owner, int(math.log2(nz))) * 2 + lax.bitwise_and(owner, 1)
        upper = lax.shift_right_logical(local, int(math.log2(cl // 2)))
        row[o] = upper * n_rows + who * (cl // 2) + lax.bitwise_and(local, cl // 2 - 1)

    def onehot(o, target):
        places = lax.broadcasted_iota(jnp.int32, (2 * n_rows, n_docs), 0)
        here = jnp.where(zpos[o, 0:1, :] == target, row[o, 0:1, :], -1)
        return (here == places).astype(jnp.float32).astype(jnp.bfloat16)

    def sums(target):
        hot = jnp.concatenate([onehot(o, target) for o in range(members)], axis=1)
        return jnp.dot(hot, docs_in[...].reshape(members * n_docs, kq), preferred_element_type=jnp.float32)

    bit = n_rows // 2
    spans = (pl.ds(0, bit + 16), pl.ds(bit + 16, bit))

    def rs_copy(way, h, p, s):
        return remote(
            rs_out.at[way, h, s, spans[p]], rs_in.at[way, h, s, spans[p]],
            rs_ss.at[way, h], rs_rs.at[way, h, p, s], z_next[way],
        )

    def rs_start(way, h, p, s, value, fine):
        values = quantise(value, fine)
        if p == 0:
            rs_out[way, h, s, 0:16] = jnp.broadcast_to(fine, (16, kq)).astype(jnp.int32).astype(jnp.int16)
            rs_out[way, h, s, 16 : bit + 16] = values
        else:
            rs_out[way, h, s, bit + 16 : 2 * bit + 16] = values
        rs_copy(way, h, p, s).start()

    def rs_send(way, h, s, value):
        fine = code(peak(value))
        for p in range(2):
            rs_start(way, h, p, s, value[p * bit : (p + 1) * bit], fine)

    def rs_fine(way, h, s):
        return rs_in[way, h, s, 0:16].astype(jnp.int32).astype(jnp.float32)[0:1]

    def rs_got(way, h, p, s, fine):
        at = 16 + p * bit
        return restore(rs_in[way, h, s, at : at + bit], fine)

    def mine(way, h):
        return acc[way, h * n_rows : (h + 1) * n_rows]

    first = [(zz + hops) % pairs, (zz + hops - 1) % pairs, (zz + pairs - hops + 1) % pairs]
    others = pl.ds(1, members - 1)
    own_ids.wait()
    all_got(ids_in.at[others], i_rs.at[0])
    for o in range(members):
        place(o)

    def arrived(o):
        if o:
            docs_copy(o).wait_recv()
        else:
            own_docs.wait()

    near = sorted(range(members), key=lambda o: (min(o // 2, ny - o // 2), o % 2))
    for o in near[:-1]:
        arrived(o)
        hot = jnp.concatenate([onehot(o, t) for t in first], axis=0)
        terms = jnp.dot(hot, docs_in[o], preferred_element_type=jnp.float32)
        for n, ref in enumerate((far, acc.at[0], acc.at[1])):
            term = terms[n * 2 * n_rows : (n + 1) * 2 * n_rows]
            ref[...] = term if o == near[0] else ref[...] + term
    o = near[-1]
    arrived(o)
    term = far[...] + jnp.dot(onehot(o, first[0]), docs_in[o], preferred_element_type=jnp.float32)
    rs_send(0, 0, 0, term[:n_rows])
    rs_send(1, 1, 0, term[n_rows:])
    for n in range(2):
        acc[n] += jnp.dot(onehot(o, first[n + 1]), docs_in[o], preferred_element_type=jnp.float32)

    for s in range(1, hops):
        for h in range(2):
            for way in range(2):
                if s == 1 and way != h:
                    rs_send(way, h, s, mine(way, h))
        chains = [(way, h) for h in range(2) for way in range(2) if s > 1 or way == h]
        tops = {(way, h): peak(mine(way, h)) for way, h in chains}
        fines = {}
        for h in range(2):
            for p in range(2):
                for way in range(2):
                    if (way, h) in tops:
                        rs_copy(way, h, p, s - 1).wait_recv()
                        before = rs_fine(way, h, s - 1)
                        if p == 0:
                            fines[way, h] = code(tops[way, h] + bound_of(before))
                        value = mine(way, h)[p * bit : (p + 1) * bit] + rs_got(way, h, p, s - 1, before)
                        rs_start(way, h, p, s, value, fines[way, h])
        if s + 1 < hops:
            acc[0] = sums((zz + hops - s - 1) % pairs)
            acc[1] = sums((zz + pairs - hops + s + 1) % pairs)
        else:
            acc[0] = sums(zz)

    quarter = members // 2

    def c_copy(h, o):
        return remote(own_cols.at[h, member(o)], cols.at[0, h, o], c_ss.at[0], c_rs.at[h, o // quarter], peer(o))

    def g_copy(way, e, d):
        if way == 0:
            src, dst = (pairs - d + 1) % pairs, pairs - d
        else:
            src, dst = d - 1, d
        h, those = e // 2, pl.ds(e % 2 * quarter, quarter)
        return remote(
            cols.at[src, h, those], cols.at[dst, h, those],
            g_ss.at[way, h], g_rs.at[way, e, d - 1], z_next[way],
        )

    own = []
    for h in range(2):
        halves = []
        for p in range(2):
            value = mine(0, h)[p * bit : (p + 1) * bit]
            for way in range(2):
                rs_copy(way, h, p, hops - 1).wait_recv()
                value = value + rs_got(way, h, p, hops - 1, rs_fine(way, h, hops - 1))
            halves.append(value)
        own.append(jnp.concatenate(halves, axis=0))
        own_cols[h] = own[h].astype(jnp.bfloat16).reshape(members, cl // 2, kq)
        for o in range(1, members):
            c_copy(h, o).start()
        cols[0, h, 0] = own_cols[h, member(0)]
    order = [value.reshape(members, nx, 8, kq) for value in own]
    rows[0] = jnp.concatenate(
        [
            order[(2 * xx + cc) // nx][m, (2 * xx + cc) % nx]
            for cc in range(2) for xx in range(nx) for m in range(members)
        ],
        axis=0,
    ).astype(jnp.bfloat16)

    def r_copy(o):
        if o == 1:
            return remote(rows.at[0], rows.at[1], r_ss.at[0], r_rs.at[0], peer(1))
        return remote(rows.at[o % 2], rows.at[o], r_ss.at[0], r_rs.at[1], peer(o - o % 2))

    r_copy(1).start()
    for o in range(2, members, 2):
        r_copy(o).start()

    for e in range(4):
        begin = max(1, e % 2 * quarter)
        all_got(cols.at[0, e // 2, pl.ds(begin, (e % 2 + 1) * quarter - begin)], c_rs.at[e // 2, e % 2])
        for way in range(2):
            g_copy(way, e, 1).start()

    def sp_copy():
        return remote(s_part.at[1 - core], s_pair_in, sp_ss.at[0], sp_rs.at[0], mate)

    def sx_copy(o):
        return remote(s_half.at[(x + o) % nx], s_x_in.at[o], sx_ss.at[0], sx_rs.at[0], x_peer(o))

    r_copy(1).wait_recv()
    for o in range(3, members, 2):
        r_copy(o).start()

    own_quer.wait()

    def wide(at):
        return jnp.concatenate(
            [jnp.concatenate([cols[at, h, o] for o in range(members)], axis=1) for h in range(2)], axis=0
        )

    asked = jnp.concatenate(
        [quer[:, pl.ds(pl.multiple_of(member_from(o) * kq, kq), kq)] for o in range(members)], axis=1
    )
    total = lax.dot_general(wide(0), asked, (((1,), (1,)), ((), ())), preferred_element_type=jnp.float32)
    total = total.reshape(nx, 2, 8, total.shape[1])
    for cc in range(2):
        for xx in range(nx):
            s_part[cc, xx] = total[xx, cc]
    sp_copy().start()

    far_x = pl.ds(1, nx - 1)
    lower = lax.broadcasted_iota(jnp.int32, (8, 2 * cl), 1) < cl

    def turn(tile):
        return pltpu.roll(tile, cl, 1)

    def p_copy(g):
        src, dst = (part.at[g], pair_in.at[g]) if g < last else (e_part.at[g - last], e_pair_in.at[g - last])
        return remote(src.at[1 - core], dst, p_ss.at[g // last], p_rs.at[g], mate)

    def x_copy(g, o):
        src, dst = (half.at[g], x_in.at[g]) if g < last else (e_half.at[g - last], e_x_in.at[g - last])
        return remote(src.at[(x + o) % nx], dst.at[o], x_ss.at[g // last], x_rs.at[g], x_peer(o))

    def f_copy(g, o):
        if g < last:
            src, dst = done.at[g, member(o)], f_in.at[g, o]
        else:
            src, dst = e_done.at[g - last, member(o) // 2], e_f_in.at[g - last, o]
        return remote(src, dst, f_ss.at[g // last], f_rs.at[g], peer(o))

    def block(g):
        these = jnp.concatenate([rows[o] for o in range(members)], axis=1)
        if g < last:
            those = jnp.concatenate([wide(pairs - g - 1), wide(g + 1)], axis=0)
        else:
            those = jnp.concatenate([wide((g - last) * hops)] * 2, axis=0)
        total = lax.dot_general(these, those, (((1,), (1,)), ((), ())), preferred_element_type=jnp.float32)
        total = total.reshape(2, nx, members, 8, 2 * cl)
        if g < last:
            part[g] = total
        else:
            two = total.reshape(2, nx, members // 2, 2, 8, 2 * cl)
            e_part[g - last] = jnp.where(lower, two[:, :, :, 0], two[:, :, :, 1])
        p_copy(g).start()

    def pair_sum(g):
        p_copy(g).wait_recv()
        if g < last:
            half[g] = part[g, core] + pair_in[g]
        else:
            e_half[g - last] = e_part[g - last, core] + e_pair_in[g - last]
        for o in range(1, nx):
            x_copy(g, o).start()

    def x_sum(g):
        mine, other = (half.at[g], x_in.at[g]) if g < last else (e_half.at[g - last], e_x_in.at[g - last])
        total = mine[x]
        all_got(other.at[far_x], x_rs.at[g])
        for o in range(1, nx):
            total = total + other[o]
        if g < last:
            done[g] = total
            f_in[g, 0] = done[g, member(0)]
        else:
            e_done[g - last] = total
            e_f_in[g - last, 0] = e_done[g - last, member(0) // 2]
        for o in range(1, members):
            f_copy(g, o).start()

    scale = 1.0 / (kd * dims)

    def store(at, tile):
        gram_ref[:, pl.ds(pl.multiple_of(at * 2 * cl, 2 * cl), 2 * cl)] = tile

    def finish(g):
        all_got((f_in.at[g] if g < last else e_f_in.at[g - last]).at[others], f_rs.at[g])
        for o in range(0, members, 2):
            at = ((y + ny - o // 2) % ny) * pairs
            same, other = (f_in[g, o], f_in[g, o + 1]) if g < last else (e_f_in[g - last, o], e_f_in[g - last, o + 1])
            even = jnp.where(zp == 0, same, other) * scale
            odd = jnp.where(zp == 0, other, same) * scale
            left = jnp.where(lower, even, turn(odd))
            right = jnp.where(lower, turn(even), odd)
            if g < last:
                store(at + (zz + pairs - g - 1) % pairs, left)
                store(at + (zz + g + 1) % pairs, right)
            else:
                store(at + (zz + (g - last) * hops) % pairs, jnp.where(zp == 0, left, right))

    before, waiting = [], []
    for d in range(1, hops + 1):
        for e in range(4):
            for way in range(2):
                if d < hops or way == e // 2:
                    g_copy(way, e, d).wait_recv()
                    if d + 1 < hops or (d + 1 == hops and way == e // 2):
                        g_copy(way, e, d + 1).start()
        if d == 1:
            all_sent(ids_in.at[others], i_ss.at[0])
            all_sent(docs_in.at[others], a_ss.at[0])
            all_sent(cols.at[0, :, others], c_ss.at[0])
            for way in range(2):
                for h in range(2):
                    begin = 0 if way == h else 1
                    all_sent(rs_out.at[way, h, pl.ds(begin, hops - begin)], rs_ss.at[way, h])
            sp_copy().wait_recv()
            s_half[...] = s_part[core] + s_pair_in[...]
            for o in range(1, nx):
                sx_copy(o).start()
        if d == min(2, last):
            all_got(rows.at[pl.ds(2, members - 2)], r_rs.at[1])
            now = [last]
        else:
            now = []
        if 2 <= d < hops:
            now.append(d - 2)
        if d == last:
            now.append(last - 1)
        if d < hops:
            for g in waiting:
                pair_sum(g)
            for g in now:
                block(g)
            before, waiting = before + waiting, now
        if d == last:
            for g in waiting:
                pair_sum(g)
    block(hops)
    before = before + waiting
    for g in before[:-1]:
        x_sum(g)
    pair_sum(hops)
    x_sum(before[-1])
    total = s_half[x]
    all_got(s_x_in.at[far_x], sx_rs.at[0])
    for o in range(1, nx):
        total = total + s_x_in[o]
    scores_ref[...] = total * ((kd * dims) ** -0.5)
    all_sent(rows.at[others], r_ss.at[0])
    for way in range(2):
        for h in range(2):
            all_sent(cols.at[pl.ds(0, hops if way == h else hops - 1), h], g_ss.at[way, h])
    sp_copy().wait_send()
    all_sent(s_x_in.at[far_x], sx_ss.at[0])
    all_sent(pair_in, p_ss.at[0])
    all_sent(x_in.at[:, far_x], x_ss.at[0])
    x_sum(hops)
    for g in before:
        finish(g)
    all_sent(e_pair_in, p_ss.at[1])
    all_sent(e_x_in.at[:, far_x], x_ss.at[1])
    all_sent(f_in.at[:, others], f_ss.at[0])
    finish(hops)
    all_sent(e_f_in.at[:, others], f_ss.at[1])


def hand_over(gram_in, scores_in, gram_ref, scores_ref):
    gram_ref[...] = gram_in[...]
    scores_ref[...] = scores_in[...]


def per_device(ny, cl, sketches, clusters, queries):
    nz = lax.axis_size("docs") // ny
    nx = lax.axis_size("dim") // 2
    n_docs, kd = sketches.shape
    nq = queries.shape[0]
    members, pairs = 2 * ny, nz // 2
    kq, rows, hops = kd // members, members * cl, pairs // 2
    last = hops - 1
    ids = clusters.reshape(1, n_docs)
    f32, bf16, i32, i16 = jnp.float32, jnp.bfloat16, jnp.int32, jnp.int16
    vmem, dma = pltpu.VMEM, pltpu.SemaphoreType.DMA
    whole = pl.BlockSpec(memory_space=pltpu.VMEM)
    away = pl.BlockSpec(memory_space=pl.ANY)
    gram, scores = pl.pallas_call(
        functools.partial(kernel, (ny, nz, nx, cl)),
        out_shape=(
            jax.ShapeDtypeStruct((8, ny * nz * cl), f32),
            jax.ShapeDtypeStruct((8, nq), f32),
        ),
        in_specs=[away, away, away],
        out_specs=(whole, whole),
        scratch_shapes=[
            vmem((members, n_docs, kq), bf16),
            vmem((members, 1, n_docs), i32),
            vmem((nq, kd), bf16),
            vmem((members, 1, n_docs), i32),
            vmem((members, 1, n_docs), i32),
            vmem((rows, kq), f32),
            vmem((2, rows, kq), f32),
            vmem((2, 2, hops, rows // 2 + 16, kq), i16),
            vmem((2, 2, hops, rows // 2 + 16, kq), i16),
            vmem((2, members, cl // 2, kq), bf16),
            vmem((pairs, 2, members, cl // 2, kq), bf16),
            vmem((members, rows, kq), bf16),
            vmem((last, 2, nx, members, 8, 2 * cl), f32),
            vmem((last, nx, members, 8, 2 * cl), f32),
            vmem((last, nx, members, 8, 2 * cl), f32),
            vmem((last, nx, members, 8, 2 * cl), f32),
            vmem((last, members, 8, 2 * cl), f32),
            vmem((last, members, 8, 2 * cl), f32),
            vmem((2, 2, nx, members // 2, 8, 2 * cl), f32),
            vmem((2, nx, members // 2, 8, 2 * cl), f32),
            vmem((2, nx, members // 2, 8, 2 * cl), f32),
            vmem((2, nx, members // 2, 8, 2 * cl), f32),
            vmem((2, members // 2, 8, 2 * cl), f32),
            vmem((2, members, 8, 2 * cl), f32),
            vmem((2, nx, 8, nq), f32),
            vmem((nx, 8, nq), f32),
            vmem((nx, 8, nq), f32),
            vmem((nx, 8, nq), f32),
            dma((3,)),
            dma((1,)), dma((members,)),
            dma((1,)), dma((1,)),
            dma((2, 2)), dma((2, 2, 2, hops)),
            dma((1,)), dma((2, 2)),
            dma((1,)), dma((2,)),
            dma((2, 2)), dma((2, 4, hops)),
            dma((2,)), dma((hops + 1,)),
            dma((2,)), dma((hops + 1,)),
            dma((2,)), dma((hops + 1,)),
            dma((1,)), dma((1,)),
            dma((1,)), dma((1,)),
        ],
        compiler_params=pltpu.CompilerParams(
            collective_id=0, has_side_effects=True, vmem_limit_bytes=56 * 1024 * 1024
        ),
    )(sketches, ids, queries)
    return pl.pallas_call(
        hand_over,
        out_shape=(
            jax.ShapeDtypeStruct((8, ny * nz * cl), f32),
            jax.ShapeDtypeStruct((8, nq), f32),
        ),
        in_specs=[whole, whole],
        out_specs=(whole, whole),
    )(gram, scores)


def solution(mesh, ny=NY, cl=CL):
    in_specs = (P("docs", "dim"), P("docs"), P(None, "dim"))
    out_specs = (P(("docs", "dim"), None), P(("docs", "dim"), None))
    return jax.shard_map(
        functools.partial(per_device, ny, cl), mesh=mesh, in_specs=in_specs, out_specs=out_specs, check_vma=False
    )
```

```python
import functools
import math

import jax
import jax.numpy as jnp
from jax import lax
from jax.experimental import pallas as pl
from jax.experimental.pallas import tpu as pltpu
from jax.sharding import PartitionSpec as P

MESH = pl.DeviceIdType.MESH
CL = 64
NY = 4
LN2 = math.log(2.0)
BITS = 15
FINE = 16


def power(level):
    return jnp.exp(level * LN2).astype(jnp.bfloat16).astype(jnp.float32)


def peak(part):
    return jnp.maximum(jnp.max(jnp.abs(part), axis=0, keepdims=True), 1e-30)


def code(bound):
    return jnp.ceil(jnp.log(bound) * (FINE / LN2) + 0.01)


def bound_of(fine):
    return jnp.exp(fine * (LN2 / FINE))


def level_of(fine):
    return jnp.floor(fine * (1.0 / FINE)) + 1.0


def quantise(part, fine):
    return jnp.round(part * power(BITS - level_of(fine))).astype(jnp.int32).astype(jnp.int16)


def restore(values, fine):
    return values.astype(jnp.int32).astype(jnp.float32) * power(level_of(fine) - BITS)


def kernel(
    sizes, sk_ref, ids_ref, qu_ref, gram_ref, scores_ref,
    docs_in, ids_in, quer, zpos, row, far, acc, rs_out, rs_in, own_cols, cols, rows,
    part, pair_in, half, x_in, done, f_in, e_part, e_pair_in, e_half, e_x_in, e_done, e_f_in,
    s_part, s_pair_in, s_half, s_x_in,
    local_sem, a_ss, a_rs, i_ss, i_rs, rs_ss, rs_rs, c_ss, c_rs, r_ss, r_rs, g_ss, g_rs,
    p_ss, p_rs, x_ss, x_rs, f_ss, f_rs, sp_ss, sp_rs, sx_ss, sx_rs,
):
    ny, nz, nx, cl = sizes
    n_docs, kd = sk_ref.shape
    members = 2 * ny
    kq = kd // members
    pairs = nz // 2
    n_rows = members * cl // 2
    hops = pairs // 2
    last = hops - 1
    dims = 2 * nx

    docs_at = lax.axis_index("docs")
    dim_at = lax.axis_index("dim")
    y, z = docs_at // nz, docs_at % nz
    zz, zp = z // 2, z % 2
    x, core = dim_at // 2, dim_at % 2

    def dev(yy, zz, zp, xx, cc):
        return (yy * nz + zz * 2 + zp, xx * 2 + cc)

    def member(o):
        return ((y + o // 2) % ny) * 2 + (zp + o % 2) % 2

    def member_from(o):
        return ((y + ny - o // 2) % ny) * 2 + (zp + o % 2) % 2

    def peer(o):
        return dev((y + o // 2) % ny, zz, (zp + o % 2) % 2, x, core)

    def x_peer(o):
        return dev(y, zz, zp, (x + o) % nx, core)

    z_next = (dev(y, (zz + 1) % pairs, zp, x, core), dev(y, (zz + pairs - 1) % pairs, zp, x, core))
    mate = dev(y, zz, zp, x, 1 - core)

    def remote(src, dst, ssem, rsem, to):
        return pltpu.make_async_remote_copy(
            src_ref=src, dst_ref=dst, send_sem=ssem, recv_sem=rsem, device_id=to, device_id_type=MESH
        )

    def all_sent(ref, sem):
        remote(ref, ref, sem, local_sem.at[0], mate).wait_send()

    def all_got(ref, sem):
        remote(ref, ref, local_sem.at[0], sem, mate).wait_recv()

    own_docs = pltpu.make_async_copy(
        sk_ref.at[:, pl.ds(pl.multiple_of(member(0) * kq, kq), kq)], docs_in.at[0], local_sem.at[0]
    )
    own_docs.start()
    own_ids = pltpu.make_async_copy(ids_ref, ids_in.at[0], local_sem.at[2])
    own_ids.start()

    barrier = pltpu.get_barrier_semaphore()
    partners = [peer(o) for o in range(1, members)] + [x_peer(o) for o in range(1, nx)] + list(z_next) + [mate]
    for to in partners:
        pl.semaphore_signal(barrier, inc=1, device_id=to, device_id_type=MESH)
    pl.semaphore_wait(barrier, len(partners))

    def ids_copy(o):
        return remote(ids_ref, ids_in.at[o], i_ss.at[0], i_rs.at[0], peer(o))

    def docs_copy(o):
        at = pl.multiple_of(member(o) * kq, kq)
        return remote(sk_ref.at[:, pl.ds(at, kq)], docs_in.at[o], a_ss.at[0], a_rs.at[o], peer(o))

    for o in range(1, members):
        ids_copy(o).start()
    for o in [1, 3, 2, 5, 4, 7, 6]:
        docs_copy(o).start()
    own_quer = pltpu.make_async_copy(qu_ref, quer, local_sem.at[1])
    own_quer.start()

    def place(o):
        ids = ids_in[o]
        owner = lax.shift_right_logical(ids, int(math.log2(cl)))
        local = lax.bitwise_and(ids, cl - 1)
        zpos[o] = lax.bitwise_and(lax.shift_right_logical(owner, 1), pairs - 1)
        who = lax.shift_right_logical(owner, int(math.log2(nz))) * 2 + lax.bitwise_and(owner, 1)
        upper = lax.shift_right_logical(local, int(math.log2(cl // 2)))
        row[o] = upper * n_rows + who * (cl // 2) + lax.bitwise_and(local, cl // 2 - 1)

    def onehot(o, target):
        places = lax.broadcasted_iota(jnp.int32, (2 * n_rows, n_docs), 0)
        here = jnp.where(zpos[o, 0:1, :] == target, row[o, 0:1, :], -1)
        return (here == places).astype(jnp.float32).astype(jnp.bfloat16)

    def sums(target):
        hot = jnp.concatenate([onehot(o, target) for o in range(members)], axis=1)
        return jnp.dot(hot, docs_in[...].reshape(members * n_docs, kq), preferred_element_type=jnp.float32)

    bit = n_rows // 2
    spans = (pl.ds(0, bit + 16), pl.ds(bit + 16, bit))

    def rs_copy(way, h, p, s):
        return remote(
            rs_out.at[way, h, s, spans[p]], rs_in.at[way, h, s, spans[p]],
            rs_ss.at[way, h], rs_rs.at[way, h, p, s], z_next[way],
        )

    def rs_start(way, h, p, s, value, fine):
        values = quantise(value, fine)
        if p == 0:
            rs_out[way, h, s, 0:16] = jnp.broadcast_to(fine, (16, kq)).astype(jnp.int32).astype(jnp.int16)
            rs_out[way, h, s, 16 : bit + 16] = values
        else:
            rs_out[way, h, s, bit + 16 : 2 * bit + 16] = values
        rs_copy(way, h, p, s).start()

    def rs_send(way, h, s, value):
        fine = code(peak(value))
        for p in range(2):
            rs_start(way, h, p, s, value[p * bit : (p + 1) * bit], fine)

    def rs_fine(way, h, s):
        return rs_in[way, h, s, 0:16].astype(jnp.int32).astype(jnp.float32)[0:1]

    def rs_got(way, h, p, s, fine):
        at = 16 + p * bit
        return restore(rs_in[way, h, s, at : at + bit], fine)

    def mine(way, h):
        return acc[way, h * n_rows : (h + 1) * n_rows]

    first = [(zz + hops) % pairs, (zz + hops - 1) % pairs, (zz + pairs - hops + 1) % pairs]
    others = pl.ds(1, members - 1)
    own_ids.wait()
    all_got(ids_in.at[others], i_rs.at[0])
    for o in range(members):
        place(o)

    def arrived(o):
        if o:
            docs_copy(o).wait_recv()
        else:
            own_docs.wait()

    near = sorted(range(members), key=lambda o: (min(o // 2, ny - o // 2), o % 2))
    for o in near[:-1]:
        arrived(o)
        hot = jnp.concatenate([onehot(o, t) for t in first], axis=0)
        terms = jnp.dot(hot, docs_in[o], preferred_element_type=jnp.float32)
        for n, ref in enumerate((far, acc.at[0], acc.at[1])):
            term = terms[n * 2 * n_rows : (n + 1) * 2 * n_rows]
            ref[...] = term if o == near[0] else ref[...] + term
    o = near[-1]
    arrived(o)
    term = far[...] + jnp.dot(onehot(o, first[0]), docs_in[o], preferred_element_type=jnp.float32)
    rs_send(0, 0, 0, term[:n_rows])
    rs_send(1, 1, 0, term[n_rows:])
    for n in range(2):
        acc[n] += jnp.dot(onehot(o, first[n + 1]), docs_in[o], preferred_element_type=jnp.float32)

    for s in range(1, hops):
        for h in range(2):
            for way in range(2):
                if s == 1 and way != h:
                    rs_send(way, h, s, mine(way, h))
        chains = [(way, h) for h in range(2) for way in range(2) if s > 1 or way == h]
        tops = {(way, h): peak(mine(way, h)) for way, h in chains}
        fines = {}
        for h in range(2):
            for p in range(2):
                for way in range(2):
                    if (way, h) in tops:
                        rs_copy(way, h, p, s - 1).wait_recv()
                        before = rs_fine(way, h, s - 1)
                        if p == 0:
                            fines[way, h] = code(tops[way, h] + bound_of(before))
                        value = mine(way, h)[p * bit : (p + 1) * bit] + rs_got(way, h, p, s - 1, before)
                        rs_start(way, h, p, s, value, fines[way, h])
        if s + 1 < hops:
            acc[0] = sums((zz + hops - s - 1) % pairs)
            acc[1] = sums((zz + pairs - hops + s + 1) % pairs)
        else:
            acc[0] = sums(zz)

    quarter = members // 2

    def c_copy(h, o):
        return remote(own_cols.at[h, member(o)], cols.at[0, h, o], c_ss.at[0], c_rs.at[h, o // quarter], peer(o))

    def g_copy(way, e, d):
        if way == 0:
            src, dst = (pairs - d + 1) % pairs, pairs - d
        else:
            src, dst = d - 1, d
        h, those = e // 2, pl.ds(e % 2 * quarter, quarter)
        return remote(
            cols.at[src, h, those], cols.at[dst, h, those],
            g_ss.at[way, h], g_rs.at[way, e, d - 1], z_next[way],
        )

    own = []
    for h in range(2):
        halves = []
        for p in range(2):
            value = mine(0, h)[p * bit : (p + 1) * bit]
            for way in range(2):
                rs_copy(way, h, p, hops - 1).wait_recv()
                value = value + rs_got(way, h, p, hops - 1, rs_fine(way, h, hops - 1))
            halves.append(value)
        own.append(jnp.concatenate(halves, axis=0))
        own_cols[h] = own[h].astype(jnp.bfloat16).reshape(members, cl // 2, kq)
        for o in range(1, members):
            c_copy(h, o).start()
        cols[0, h, 0] = own_cols[h, member(0)]
    order = [value.reshape(members, nx, 8, kq) for value in own]
    rows[0] = jnp.concatenate(
        [
            order[(2 * xx + cc) // nx][m, (2 * xx + cc) % nx]
            for cc in range(2) for xx in range(nx) for m in range(members)
        ],
        axis=0,
    ).astype(jnp.bfloat16)

    def r_copy(o):
        if o == 1:
            return remote(rows.at[0], rows.at[1], r_ss.at[0], r_rs.at[0], peer(1))
        return remote(rows.at[o % 2], rows.at[o], r_ss.at[0], r_rs.at[1], peer(o - o % 2))

    r_copy(1).start()
    for o in range(2, members, 2):
        r_copy(o).start()

    for e in range(4):
        begin = max(1, e % 2 * quarter)
        all_got(cols.at[0, e // 2, pl.ds(begin, (e % 2 + 1) * quarter - begin)], c_rs.at[e // 2, e % 2])
        for way in range(2):
            g_copy(way, e, 1).start()

    def sp_copy():
        return remote(s_part.at[1 - core], s_pair_in, sp_ss.at[0], sp_rs.at[0], mate)

    def sx_copy(o):
        return remote(s_half.at[(x + o) % nx], s_x_in.at[o], sx_ss.at[0], sx_rs.at[0], x_peer(o))

    r_copy(1).wait_recv()
    for o in range(3, members, 2):
        r_copy(o).start()

    own_quer.wait()

    def wide(at):
        return jnp.concatenate(
            [jnp.concatenate([cols[at, h, o] for o in range(members)], axis=1) for h in range(2)], axis=0
        )

    asked = jnp.concatenate(
        [quer[:, pl.ds(pl.multiple_of(member_from(o) * kq, kq), kq)] for o in range(members)], axis=1
    )
    total = lax.dot_general(wide(0), asked, (((1,), (1,)), ((), ())), preferred_element_type=jnp.float32)
    total = total.reshape(nx, 2, 8, total.shape[1])
    for cc in range(2):
        for xx in range(nx):
            s_part[cc, xx] = total[xx, cc]
    sp_copy().start()

    far_x = pl.ds(1, nx - 1)
    lower = lax.broadcasted_iota(jnp.int32, (8, 2 * cl), 1) < cl

    def turn(tile):
        return pltpu.roll(tile, cl, 1)

    def p_copy(g):
        src, dst = (part.at[g], pair_in.at[g]) if g < last else (e_part.at[g - last], e_pair_in.at[g - last])
        return remote(src.at[1 - core], dst, p_ss.at[g // last], p_rs.at[g], mate)

    def x_copy(g, o):
        src, dst = (half.at[g], x_in.at[g]) if g < last else (e_half.at[g - last], e_x_in.at[g - last])
        return remote(src.at[(x + o) % nx], dst.at[o], x_ss.at[g // last], x_rs.at[g], x_peer(o))

    def f_copy(g, o):
        if g < last:
            src, dst = done.at[g, member(o)], f_in.at[g, o]
        else:
            src, dst = e_done.at[g - last, member(o) // 2], e_f_in.at[g - last, o]
        return remote(src, dst, f_ss.at[g // last], f_rs.at[g], peer(o))

    def block(g):
        these = jnp.concatenate([rows[o] for o in range(members)], axis=1)
        if g < last:
            those = jnp.concatenate([wide(pairs - g - 1), wide(g + 1)], axis=0)
        else:
            those = jnp.concatenate([wide((g - last) * hops)] * 2, axis=0)
        total = lax.dot_general(these, those, (((1,), (1,)), ((), ())), preferred_element_type=jnp.float32)
        total = total.reshape(2, nx, members, 8, 2 * cl)
        if g < last:
            part[g] = total
        else:
            two = total.reshape(2, nx, members // 2, 2, 8, 2 * cl)
            e_part[g - last] = jnp.where(lower, two[:, :, :, 0], two[:, :, :, 1])
        p_copy(g).start()

    def pair_sum(g):
        p_copy(g).wait_recv()
        if g < last:
            half[g] = part[g, core] + pair_in[g]
        else:
            e_half[g - last] = e_part[g - last, core] + e_pair_in[g - last]
        for o in range(1, nx):
            x_copy(g, o).start()

    def x_sum(g):
        mine, other = (half.at[g], x_in.at[g]) if g < last else (e_half.at[g - last], e_x_in.at[g - last])
        total = mine[x]
        all_got(other.at[far_x], x_rs.at[g])
        for o in range(1, nx):
            total = total + other[o]
        if g < last:
            done[g] = total
            f_in[g, 0] = done[g, member(0)]
        else:
            e_done[g - last] = total
            e_f_in[g - last, 0] = e_done[g - last, member(0) // 2]
        for o in range(1, members):
            f_copy(g, o).start()

    scale = 1.0 / (kd * dims)

    def store(at, tile):
        gram_ref[:, pl.ds(pl.multiple_of(at * 2 * cl, 2 * cl), 2 * cl)] = tile

    def finish(g):
        all_got((f_in.at[g] if g < last else e_f_in.at[g - last]).at[others], f_rs.at[g])
        for o in range(0, members, 2):
            at = ((y + ny - o // 2) % ny) * pairs
            same, other = (f_in[g, o], f_in[g, o + 1]) if g < last else (e_f_in[g - last, o], e_f_in[g - last, o + 1])
            even = jnp.where(zp == 0, same, other) * scale
            odd = jnp.where(zp == 0, other, same) * scale
            left = jnp.where(lower, even, turn(odd))
            right = jnp.where(lower, turn(even), odd)
            if g < last:
                store(at + (zz + pairs - g - 1) % pairs, left)
                store(at + (zz + g + 1) % pairs, right)
            else:
                store(at + (zz + (g - last) * hops) % pairs, jnp.where(zp == 0, left, right))

    before, waiting = [], []
    for d in range(1, hops + 1):
        for e in range(4):
            for way in range(2):
                if d < hops or way == e // 2:
                    g_copy(way, e, d).wait_recv()
                    if d + 1 < hops or (d + 1 == hops and way == e // 2):
                        g_copy(way, e, d + 1).start()
        if d == 1:
            all_sent(ids_in.at[others], i_ss.at[0])
            all_sent(docs_in.at[others], a_ss.at[0])
            all_sent(cols.at[0, :, others], c_ss.at[0])
            for way in range(2):
                for h in range(2):
                    begin = 0 if way == h else 1
                    all_sent(rs_out.at[way, h, pl.ds(begin, hops - begin)], rs_ss.at[way, h])
            sp_copy().wait_recv()
            s_half[...] = s_part[core] + s_pair_in[...]
            for o in range(1, nx):
                sx_copy(o).start()
        if d == min(2, last):
            all_got(rows.at[pl.ds(2, members - 2)], r_rs.at[1])
            now = [last]
        else:
            now = []
        if 2 <= d < hops:
            now.append(d - 2)
        if d == last:
            now.append(last - 1)
        if d < hops:
            for g in waiting:
                pair_sum(g)
            for g in now:
                block(g)
            before, waiting = before + waiting, now
        if d == last:
            for g in waiting:
                pair_sum(g)
            for g in before:
                x_sum(g)
    block(hops)
    pair_sum(hops)
    for g in waiting:
        x_sum(g)
    before = before + waiting
    total = s_half[x]
    all_got(s_x_in.at[far_x], sx_rs.at[0])
    for o in range(1, nx):
        total = total + s_x_in[o]
    scores_ref[...] = total * ((kd * dims) ** -0.5)
    all_sent(rows.at[others], r_ss.at[0])
    for way in range(2):
        for h in range(2):
            all_sent(cols.at[pl.ds(0, hops if way == h else hops - 1), h], g_ss.at[way, h])
    sp_copy().wait_send()
    all_sent(s_x_in.at[far_x], sx_ss.at[0])
    all_sent(pair_in, p_ss.at[0])
    all_sent(x_in.at[:, far_x], x_ss.at[0])
    x_sum(hops)
    for g in before:
        finish(g)
    all_sent(e_pair_in, p_ss.at[1])
    all_sent(e_x_in.at[:, far_x], x_ss.at[1])
    all_sent(f_in.at[:, others], f_ss.at[0])
    finish(hops)
    all_sent(e_f_in.at[:, others], f_ss.at[1])


def hand_over(gram_in, scores_in, gram_ref, scores_ref):
    gram_ref[...] = gram_in[...]
    scores_ref[...] = scores_in[...]


def per_device(ny, cl, sketches, clusters, queries):
    nz = lax.axis_size("docs") // ny
    nx = lax.axis_size("dim") // 2
    n_docs, kd = sketches.shape
    nq = queries.shape[0]
    members, pairs = 2 * ny, nz // 2
    kq, rows, hops = kd // members, members * cl, pairs // 2
    last = hops - 1
    ids = clusters.reshape(1, n_docs)
    f32, bf16, i32, i16 = jnp.float32, jnp.bfloat16, jnp.int32, jnp.int16
    vmem, dma = pltpu.VMEM, pltpu.SemaphoreType.DMA
    whole = pl.BlockSpec(memory_space=pltpu.VMEM)
    away = pl.BlockSpec(memory_space=pl.ANY)
    gram, scores = pl.pallas_call(
        functools.partial(kernel, (ny, nz, nx, cl)),
        out_shape=(
            jax.ShapeDtypeStruct((8, ny * nz * cl), f32),
            jax.ShapeDtypeStruct((8, nq), f32),
        ),
        in_specs=[away, away, away],
        out_specs=(whole, whole),
        scratch_shapes=[
            vmem((members, n_docs, kq), bf16),
            vmem((members, 1, n_docs), i32),
            vmem((nq, kd), bf16),
            vmem((members, 1, n_docs), i32),
            vmem((members, 1, n_docs), i32),
            vmem((rows, kq), f32),
            vmem((2, rows, kq), f32),
            vmem((2, 2, hops, rows // 2 + 16, kq), i16),
            vmem((2, 2, hops, rows // 2 + 16, kq), i16),
            vmem((2, members, cl // 2, kq), bf16),
            vmem((pairs, 2, members, cl // 2, kq), bf16),
            vmem((members, rows, kq), bf16),
            vmem((last, 2, nx, members, 8, 2 * cl), f32),
            vmem((last, nx, members, 8, 2 * cl), f32),
            vmem((last, nx, members, 8, 2 * cl), f32),
            vmem((last, nx, members, 8, 2 * cl), f32),
            vmem((last, members, 8, 2 * cl), f32),
            vmem((last, members, 8, 2 * cl), f32),
            vmem((2, 2, nx, members // 2, 8, 2 * cl), f32),
            vmem((2, nx, members // 2, 8, 2 * cl), f32),
            vmem((2, nx, members // 2, 8, 2 * cl), f32),
            vmem((2, nx, members // 2, 8, 2 * cl), f32),
            vmem((2, members // 2, 8, 2 * cl), f32),
            vmem((2, members, 8, 2 * cl), f32),
            vmem((2, nx, 8, nq), f32),
            vmem((nx, 8, nq), f32),
            vmem((nx, 8, nq), f32),
            vmem((nx, 8, nq), f32),
            dma((3,)),
            dma((1,)), dma((members,)),
            dma((1,)), dma((1,)),
            dma((2, 2)), dma((2, 2, 2, hops)),
            dma((1,)), dma((2, 2)),
            dma((1,)), dma((2,)),
            dma((2, 2)), dma((2, 4, hops)),
            dma((2,)), dma((hops + 1,)),
            dma((2,)), dma((hops + 1,)),
            dma((2,)), dma((hops + 1,)),
            dma((1,)), dma((1,)),
            dma((1,)), dma((1,)),
        ],
        compiler_params=pltpu.CompilerParams(
            collective_id=0, has_side_effects=True, vmem_limit_bytes=56 * 1024 * 1024
        ),
    )(sketches, ids, queries)
    return pl.pallas_call(
        hand_over,
        out_shape=(
            jax.ShapeDtypeStruct((8, ny * nz * cl), f32),
            jax.ShapeDtypeStruct((8, nq), f32),
        ),
        in_specs=[whole, whole],
        out_specs=(whole, whole),
    )(gram, scores)


def solution(mesh, ny=NY, cl=CL):
    in_specs = (P("docs", "dim"), P("docs"), P(None, "dim"))
    out_specs = (P(("docs", "dim"), None), P(("docs", "dim"), None))
    return jax.shard_map(
        functools.partial(per_device, ny, cl), mesh=mesh, in_specs=in_specs, out_specs=out_specs, check_vma=False
    )
```
